32 devices in a mesh: dp: 8 (over z, x), mp: 4 (over y, core).
Axes of the slice: x: 2, y: 2, z: 4, core: 2. Of those that a mesh axis runs over, the one named last changes fastest.
Arguments:
- input_steps: bfloat16 [4, 768, 8192], P(None, 'dp', 'mp'), may hold values from -6 to 6
- gate_steps: bfloat16 [4, 768, 8192], P(None, 'dp', 'mp'), may hold values from -6 to 6
- conv_state: bfloat16 [768, 3, 8192], P('dp', None, 'mp'), may hold values from -6 to 6
- ssm_state: bfloat16 [768, 16, 8192], P('dp', None, 'mp'), may hold values from -6 to 6
- new_slot: int32 [768], replicated, may hold values from 0 to 767, as said below
- remaining: int32 [768], replicated, may hold values from 1 to 4
- conv_weight: float32 [4, 8192], P(None, 'mp'), may hold values from -3 to 3
- conv_bias: float32 [8192], P('mp'), may hold values from -3 to 3
- coef_proj: bfloat16 [8192, 544], P('mp', 'dp'), may hold values from -0.0625 to 0.0625
- delta_proj: bfloat16 [512, 8192], P('dp', 'mp'), may hold values from -0.25 to 0.25
- delta_bias: float32 [8192], P('mp'), may hold values from -4 to -1
- decay_log: float32 [16, 8192], P(None, 'mp'), may hold values from -1 to 2
- skip_gain: float32 [8192], P('mp'), may hold values from 0.5 to 1.5
- out_proj: bfloat16 [8192, 4096], P('mp', 'dp'), may hold values from -0.0625 to 0.0625
Outputs:
- layer_out: bfloat16 [4, 768, 4096], P(None, 'dp', 'mp')
- conv_final: bfloat16 [768, 3, 8192], P('dp', None, 'mp')
- ssm_final: bfloat16 [768, 16, 8192], P('dp', None, 'mp')
The draws below stay inside these ranges and needn't reach their ends.
Inputs may be any that keep to these rules, and one draw needn't show every extreme that they name: new_slot is a permutation of the rollouts. Each group hands to every group 0, 12 or 24 of its rollouts: 24 to exactly one group and 0 to exactly one group; each group receives 24 from exactly one group and 0 from exactly one group.
All inputs are finite; a program needn't handle non-finite values.
Results may differ from the reference program's by a relative error of at most 0.03.
Values may be sent and summed in bfloat16 or wider, within the bound.
A program may use at most 128 MiB of HBM per device.

```python
import jax
import jax.numpy as jnp
from jax import lax

E_WIN = 8192
D_OUT = 4096
DT_RANK = 512
STATE = 16
TAPS = 4
STEPS = 4
ROWS = 96
TOTAL = 768
N_DP = 8
N_MP = 4


def draw_new_slot(key, part):
    groups = N_DP
    base = ROWS // N_DP
    base_key = jax.random.fold_in(key, 7)
    key_sigma, key_order, key_within = jax.random.split(base_key, 3)
    sigma = jax.random.permutation(key_sigma, groups).astype(jnp.int32)
    tau = jnp.roll(sigma, -1)
    column = jnp.arange(groups, dtype=jnp.int32)
    counts = base + base * (column[None, :] == sigma[:, None]).astype(jnp.int32) - base * (column[None, :] == tau[:, None]).astype(jnp.int32)
    cumulative = jnp.cumsum(counts, axis=1)
    position = jnp.arange(ROWS, dtype=jnp.int32)
    target = jnp.sum((cumulative[:, None, :] <= position[None, :, None]).astype(jnp.int32), axis=2)
    start_source = cumulative - counts
    before = jnp.cumsum(counts, axis=0) - counts
    offset = jnp.take_along_axis(before, target, axis=1) + position[None, :] - jnp.take_along_axis(start_source, target, axis=1)
    within_keys = jax.random.split(key_within, groups)
    shuffles = jax.vmap(lambda sub_key: jax.random.permutation(sub_key, ROWS).astype(jnp.int32))(within_keys)
    final_slot = shuffles[target.reshape(-1), offset.reshape(-1)].reshape(groups, ROWS)
    values = target * ROWS + final_slot
    order_keys = jax.random.split(key_order, groups)
    orders = jax.vmap(lambda sub_key: jax.random.permutation(sub_key, ROWS).astype(jnp.int32))(order_keys)
    group_index = jnp.broadcast_to(column[:, None], (groups, ROWS))
    result = jnp.zeros((groups, ROWS), jnp.int32).at[group_index, orders].set(values)
    return result.reshape(groups * ROWS)


def set_ends(values, own_key, least, high):
    longest = values.shape.index(max(values.shape))
    spots = []
    for shift in (0, 1):
        where = [jax.random.randint(jax.random.fold_in(own_key, axis), (), 0, length) for axis, length in enumerate(values.shape)]
        where[longest] = (where[longest] + shift) % values.shape[longest]
        spots.append(tuple(where))
    return values.at[spots[0]].set(least).at[spots[1]].set(high)


def levels(own_key, extent, shards, least, high):
    level = 1.0
    for dim, shards_of in shards:
        steps = jax.random.uniform(jax.random.fold_in(jax.random.fold_in(own_key, 6), dim), (shards_of,), jnp.float32, least / len(shards), high / len(shards))
        level = level * jnp.repeat(jnp.exp(steps), extent[dim] // shards_of).reshape((-1,) + (1,) * (len(extent) - 1 - dim))
    return level


def scatter_about(own_key, shape, scale, most, cuts=(), kind=jnp.bfloat16):
    array = scale * jax.random.normal(own_key, shape, jnp.float32)
    if cuts:
        array = array * levels(own_key, shape, cuts, -0.22, 0.18)
    return jnp.clip(array, -most, most).astype(kind)


def setup_inputs(seed: int = 0) -> dict:
    key_list = jax.random.split(jax.random.key(seed), 15)
    return {
        "input_steps": scatter_about(key_list[0], (STEPS, TOTAL, E_WIN), 1.0, 6.0, ((1, 8), (2, 4))),
        "gate_steps": scatter_about(key_list[1], (STEPS, TOTAL, E_WIN), 1.0, 6.0, ((1, 8), (2, 4))),
        "conv_state": scatter_about(key_list[2], (TOTAL, TAPS - 1, E_WIN), 1.0, 6.0, ((0, 8), (2, 4))),
        "ssm_state": scatter_about(key_list[3], (TOTAL, STATE, E_WIN), 1.0, 6.0, ((0, 8), (2, 4))),
        "new_slot": draw_new_slot(jax.random.fold_in(key_list[14], 71), 0),
        "remaining": set_ends(jax.random.randint(key_list[5], (TOTAL,), 1, STEPS + 1), jax.random.fold_in(key_list[5], 1), 1, STEPS).astype(jnp.int32),
        "conv_weight": scatter_about(key_list[6], (TAPS, E_WIN), 0.5, 3.0, ((1, 4),), jnp.float32),
        "conv_bias": scatter_about(key_list[7], (E_WIN,), 0.5, 3.0, ((0, 4),), jnp.float32),
        "coef_proj": scatter_about(key_list[8], (E_WIN, DT_RANK + 2 * STATE), E_WIN ** -0.5, 0.0625, ((0, 4), (1, 8))),
        "delta_proj": scatter_about(key_list[9], (DT_RANK, E_WIN), DT_RANK ** -0.5, 0.25, ((0, 8), (1, 4))),
        "delta_bias": jnp.clip(-4.0 + 3.0 * jax.random.uniform(key_list[10], (E_WIN,), jnp.float32) ** levels(key_list[10], (E_WIN,), ((0, 4),), -0.2, 0.2), -4.0, -1.0),
        "decay_log": jnp.clip(-1.0 + 3.0 * jax.random.uniform(key_list[11], (STATE, E_WIN), jnp.float32) ** levels(key_list[11], (STATE, E_WIN), ((1, 4),), -0.2, 0.2), -1.0, 2.0),
        "skip_gain": jnp.clip(0.5 + 1.0 * jax.random.uniform(key_list[12], (E_WIN,), jnp.float32) ** levels(key_list[12], (E_WIN,), ((0, 4),), -0.2, 0.2), 0.5, 1.5),
        "out_proj": scatter_about(key_list[13], (E_WIN, D_OUT), E_WIN ** -0.5, 0.0625, ((0, 4), (1, 8))),
    }


def reference(input_steps, gate_steps, conv_state, ssm_state, new_slot, remaining, conv_weight, conv_bias, coef_proj, delta_proj, delta_bias, decay_log, skip_gain, out_proj):
    total_rows = new_slot.shape[0]
    channels = input_steps.shape[2]
    inverse = jnp.zeros((total_rows,), jnp.int32).at[new_slot].set(jnp.arange(total_rows, dtype=jnp.int32))
    conv_moved = conv_state[inverse]
    ssm_moved = ssm_state[inverse]
    remain_moved = remaining[inverse]
    decay_rate = -jnp.exp(decay_log)
    inputs = (
        input_steps.reshape(STEPS, N_DP, ROWS, channels).transpose(1, 0, 2, 3),
        gate_steps.reshape(STEPS, N_DP, ROWS, channels).transpose(1, 0, 2, 3),
        conv_moved.reshape(N_DP, ROWS, TAPS - 1, channels),
        ssm_moved.reshape(N_DP, ROWS, STATE, channels),
        remain_moved.reshape(N_DP, ROWS),
    )

    def advance(group_rows):
        input_group, gate_group, window_in, state_in, remain_group = group_rows
        window = window_in.astype(jnp.float32)
        hidden = state_in.astype(jnp.float32)
        results = []
        for position in range(STEPS):
            active = (remain_group > position)[:, None]
            current = input_group[position].astype(jnp.float32)
            full_window = jnp.concatenate([window, current[:, None, :]], axis=1)
            conv_out = jnp.sum(full_window * conv_weight[None], axis=1) + conv_bias
            activated = jax.nn.silu(conv_out)
            low_rank = jnp.dot(activated.astype(jnp.bfloat16), coef_proj, preferred_element_type=jnp.float32)
            step_in = low_rank[:, :DT_RANK].astype(jnp.bfloat16)
            input_coef = low_rank[:, DT_RANK:DT_RANK + STATE]
            output_coef = low_rank[:, DT_RANK + STATE:]
            step_size = jax.nn.softplus(jnp.dot(step_in, delta_proj, preferred_element_type=jnp.float32) + delta_bias)
            decay_factor = jnp.exp(step_size[:, None, :] * decay_rate[None])
            updated = decay_factor * hidden + (step_size * activated)[:, None, :] * input_coef[:, :, None]
            mixer = (jnp.sum(updated * output_coef[:, :, None], axis=1) + skip_gain * activated) * jax.nn.silu(gate_group[position].astype(jnp.float32))
            hidden = jnp.where(active[:, :, None], updated, hidden)
            window = jnp.where(active[:, :, None], full_window[:, 1:], window)
            results.append(jnp.where(active, mixer, 0.0).astype(jnp.bfloat16))
        stacked = jnp.stack(results).reshape(STEPS * ROWS, channels)
        pieces = jnp.einsum(
            "rge,ged->grd",
            stacked.reshape(STEPS * ROWS, N_MP, channels // N_MP).astype(jnp.float32),
            out_proj.reshape(N_MP, channels // N_MP, D_OUT).astype(jnp.float32),
        )
        rounded = lax.optimization_barrier(pieces.astype(jnp.bfloat16))
        layer_block = jnp.sum(rounded.astype(jnp.float32), axis=0).astype(jnp.bfloat16)
        return layer_block.reshape(STEPS, ROWS, D_OUT), window.astype(jnp.bfloat16), hidden.astype(jnp.bfloat16)

    layer_out, conv_final, ssm_final = lax.map(advance, inputs)
    layer_out = layer_out.transpose(1, 0, 2, 3).reshape(STEPS, total_rows, D_OUT)
    return layer_out, conv_final.reshape(total_rows, TAPS - 1, channels), ssm_final.reshape(total_rows, STATE, channels)
```

```python
import jax
import jax.numpy as jnp
from jax import lax
from jax.experimental import pallas as pl
from jax.experimental.pallas import tpu as pltpu
from jax.sharding import PartitionSpec as P

VMEM_LIMIT = 48 * 1024 * 1024


def pack_kernel(index_ref, state_ref, base_ref, extra_ref):
    block = pl.program_id(0)
    cap = base_ref.shape[0]
    blocks = pl.num_programs(0)
    for i in range(cap):
        base_ref[i] = state_ref[index_ref[block * cap + i]]

    @pl.when(block == 0)
    def _():
        for i in range(cap):
            extra_ref[i] = state_ref[index_ref[blocks * cap + i]]


def pack(index, state, groups):
    rows, depth, channels = state.shape
    cap = rows // groups
    return pl.pallas_call(
        pack_kernel,
        out_shape=(
            jax.ShapeDtypeStruct((rows, depth, channels), state.dtype),
            jax.ShapeDtypeStruct((cap, depth, channels), state.dtype),
        ),
        grid_spec=pltpu.PrefetchScalarGridSpec(
            num_scalar_prefetch=1,
            grid=(groups,),
            in_specs=[
                pl.BlockSpec((rows, depth, channels), lambda i, _: (0, 0, 0)),
            ],
            out_specs=(
                pl.BlockSpec((cap, depth, channels), lambda i, _: (i, 0, 0)),
                pl.BlockSpec((cap, depth, channels), lambda i, _: (0, 0, 0)),
            ),
        ),
        compiler_params=pltpu.CompilerParams(vmem_limit_bytes=VMEM_LIMIT),
        cost_estimate=pl.CostEstimate(
            flops=0, bytes_accessed=4 * state.size, transcendentals=0
        ),
    )(index, state)


def scan_kernel(
    slot_ref,
    base_ref,
    extra_ref,
    step_ref,
    act_ref,
    gate_ref,
    coef_ref,
    mask_ref,
    decay_ref,
    skip_ref,
    mix_ref,
    final_ref,
    read_ref,
):
    first = pl.program_id(0) * step_ref.shape[1]
    rows_total = base_ref.shape[0]
    steps, rows, channels = step_ref.shape
    width = min(512, channels)

    def one_row(r, carry):
        slot = slot_ref[first + r]
        in_base = slot < rows_total
        at_base = jnp.minimum(slot, rows_total - 1)
        at_extra = jnp.maximum(slot - rows_total, 0)
        coef = coef_ref[r]
        for c in range(0, channels, width):
            cols = pl.ds(c, width)
            hidden = jnp.where(
                in_base,
                base_ref[at_base, :, cols].astype(jnp.float32),
                extra_ref[at_extra, :, cols].astype(jnp.float32),
            )
            decay = decay_ref[:, cols]
            for t in range(steps):
                step = step_ref[t, pl.ds(r, 1), cols]
                act = act_ref[t, pl.ds(r, 1), cols]
                hidden = (
                    jnp.exp(step * decay) * hidden + (step * act) * coef[:, 2 * t : 2 * t + 1]
                )
                read_ref[t, pl.ds(r, 1), cols] = jnp.sum(
                    hidden * coef[:, 2 * t + 1 : 2 * t + 2], axis=0, keepdims=True
                )
            final_ref[r, :, cols] = hidden.astype(final_ref.dtype)
        return carry

    lax.fori_loop(0, rows, one_row, 0)
    for t in range(steps):
        gate = gate_ref[t].astype(jnp.float32)
        mixer = (read_ref[t] + skip_ref[...] * act_ref[t]) * jax.nn.silu(gate)
        mix_ref[t] = jnp.where(mask_ref[:, t : t + 1] > 0, mixer, 0.0).astype(mix_ref.dtype)


def scan(slot, base, extra, step, act, gate, coef, mask, decay, skip):
    rows, depth, channels = base.shape
    steps = step.shape[0]
    tile = 16
    cap = extra.shape[0]

    def whole(shape):
        return pl.BlockSpec(shape, lambda i, _: (0,) * len(shape))

    per_step = pl.BlockSpec((steps, tile, channels), lambda i, _: (0, i, 0))
    return pl.pallas_call(
        scan_kernel,
        out_shape=(
            jax.ShapeDtypeStruct((steps, rows, channels), jnp.bfloat16),
            jax.ShapeDtypeStruct((rows, depth, channels), jnp.bfloat16),
        ),
        grid_spec=pltpu.PrefetchScalarGridSpec(
            num_scalar_prefetch=1,
            grid=(rows // tile,),
            in_specs=[
                whole((rows, depth, channels)),
                whole((cap, depth, channels)),
                per_step,
                per_step,
                per_step,
                pl.BlockSpec((tile, depth, 2 * steps), lambda i, _: (i, 0, 0)),
                pl.BlockSpec((tile, steps), lambda i, _: (i, 0)),
                whole((depth, channels)),
                whole((1, channels)),
            ],
            out_specs=(
                per_step,
                pl.BlockSpec((tile, depth, channels), lambda i, _: (i, 0, 0)),
            ),
            scratch_shapes=[pltpu.VMEM((steps, tile, channels), jnp.float32)],
        ),
        compiler_params=pltpu.CompilerParams(vmem_limit_bytes=VMEM_LIMIT),
        cost_estimate=pl.CostEstimate(
            flops=8 * steps * base.size,
            bytes_accessed=4 * base.size + 16 * step.size,
            transcendentals=steps * base.size,
        ),
    )(slot, base, extra, step, act, gate, coef, mask, decay, skip)


def per_device(
    input_steps,
    gate_steps,
    conv_state,
    ssm_state,
    new_slot,
    remaining,
    conv_weight,
    conv_bias,
    coef_proj,
    delta_proj,
    delta_bias,
    decay_log,
    skip_gain,
    out_proj,
):
    groups = lax.axis_size("dp")
    my_group = lax.axis_index("dp")
    row_count, taps_kept, channels = conv_state.shape
    state_len = ssm_state.shape[1]
    steps_total = input_steps.shape[0]
    cap = row_count // groups
    total_rows = new_slot.shape[0]

    target = (new_slot // row_count).reshape(groups, row_count)
    position = jnp.arange(row_count, dtype=jnp.int32)
    earlier = position[None, :] < position[:, None]
    rank = jnp.sum(
        ((target[:, :, None] == target[:, None, :]) & earlier[None]).astype(jnp.int32), axis=2
    )
    source = jnp.broadcast_to(jnp.arange(groups, dtype=jnp.int32)[:, None], rank.shape)
    my_target = lax.dynamic_index_in_dim(target, my_group, 0, keepdims=False)
    my_rank = lax.dynamic_index_in_dim(rank, my_group, 0, keepdims=False)
    leave = jnp.where(
        my_rank < cap, my_target * cap + my_rank, row_count + my_rank - cap
    )
    slots = jnp.arange(row_count + cap, dtype=jnp.int32)
    send_index = jnp.sum(
        jnp.where(slots[:, None] == leave[None, :], position[None, :], 0), axis=1
    )
    arrive = jnp.where(rank < cap, source * cap + rank, row_count + rank - cap)
    here = (new_slot[None, :] == (my_group * row_count + position)[:, None])
    slot = jnp.sum(jnp.where(here, arrive.reshape(1, total_rows), 0), axis=1)
    remain_new = jnp.sum(jnp.where(here, remaining[None, :], 0), axis=1)
    group_ids = jnp.arange(groups, dtype=jnp.int32)
    is_extra = (rank == cap).reshape(1, total_rows)
    extra_from = jnp.sum(
        jnp.where(
            is_extra & (target.reshape(1, total_rows) == group_ids[:, None]),
            source.reshape(1, total_rows),
            0,
        ),
        axis=1,
    )

    def exchange(block):
        return lax.all_to_all(block, "dp", split_axis=0, concat_axis=0, tiled=True)

    ssm_base, ssm_extra = pack(send_index, ssm_state, groups)
    conv_packed = conv_state[send_index]
    extra = jnp.concatenate([ssm_extra, conv_packed[row_count:]], axis=1)
    extra = extra.reshape(cap, state_len + taps_kept, groups, channels // groups)
    extra = exchange(extra.transpose(2, 0, 1, 3))
    extra = exchange(extra[extra_from])
    extra = extra.transpose(1, 2, 0, 3).reshape(cap, state_len + taps_kept, channels)
    conv_base = exchange(conv_packed[:row_count])
    ssm_base = exchange(ssm_base)
    ssm_extra = extra[:, :state_len]

    small = jnp.concatenate([coef_proj.T, delta_proj], axis=0)
    small = lax.all_gather(small, "dp", axis=0, tiled=False)
    coef_width = coef_proj.shape[1]
    coef_whole = small[:, :coef_width].reshape(groups * coef_width, channels)
    delta_whole = small[:, coef_width:].reshape(-1, channels)
    rank_len = delta_whole.shape[0]
    out_whole = lax.all_gather(out_proj, "dp", axis=0, tiled=False)

    conv_moved = jnp.concatenate([conv_base, extra[:, state_len:]], axis=0)[slot]
    sequence = [conv_moved[:, k] for k in range(taps_kept)]
    sequence += [input_steps[t] for t in range(steps_total)]
    wide = [entry.astype(jnp.float32) for entry in sequence]
    activated = jnp.stack(
        [
            jax.nn.silu(
                sum(wide[t + k] * conv_weight[k][None] for k in range(taps_kept + 1)) + conv_bias
            )
            for t in range(steps_total)
        ]
    )
    partial_value = lax.dot_general(
        activated.reshape(steps_total * row_count, channels).astype(jnp.bfloat16),
        coef_whole,
        (((1,), (1,)), ((), ())),
        preferred_element_type=jnp.float32,
    )
    low_rank = lax.psum(partial_value.astype(jnp.bfloat16), "mp")
    coef = low_rank[:, rank_len:].astype(jnp.float32)
    coef = coef.reshape(steps_total, row_count, 2, state_len)
    coef = coef.transpose(1, 3, 0, 2).reshape(row_count, state_len, 2 * steps_total)
    active = remain_new[:, None] > jnp.arange(steps_total, dtype=jnp.int32)[None, :]
    step_size = jax.nn.softplus(
        jnp.dot(low_rank[:, :rank_len], delta_whole, preferred_element_type=jnp.float32)
        + delta_bias
    ).reshape(steps_total, row_count, channels)
    step_size = jnp.where(active.T[:, :, None], step_size, 0.0)

    mixed, ssm_final = scan(
        slot,
        ssm_base,
        ssm_extra,
        step_size,
        activated,
        gate_steps,
        coef,
        active.astype(jnp.int32),
        -jnp.exp(decay_log),
        skip_gain[None],
    )
    last = jnp.minimum(remain_new, steps_total)[:, None]
    window = []
    for k in range(taps_kept):
        entry = sequence[k]
        for t in range(1, steps_total + 1):
            entry = jnp.where(last == t, sequence[k + t], entry)
        window.append(entry)
    conv_final = jnp.stack(window, axis=1)

    partial_mix = jnp.einsum(
        "rc,gcd->rgd",
        mixed.reshape(steps_total * row_count, channels),
        out_whole,
        preferred_element_type=jnp.float32,
    ).reshape(steps_total * row_count, -1)
    summed = lax.psum_scatter(
        partial_mix.astype(jnp.bfloat16), "mp", scatter_dimension=1, tiled=True
    )
    layer_out = summed.reshape(steps_total, row_count, summed.shape[1])
    return (layer_out, conv_final, ssm_final)


def solution(mesh):
    return jax.shard_map(
        per_device,
        mesh=mesh,
        in_specs=(
            P(None, "dp", "mp"),
            P(None, "dp", "mp"),
            P("dp", None, "mp"),
            P("dp", None, "mp"),
            P(),
            P(),
            P(None, "mp"),
            P("mp"),
            P("mp", "dp"),
            P("dp", "mp"),
            P("mp"),
            P(None, "mp"),
            P("mp"),
            P("mp", "dp"),
        ),
        out_specs=(P(None, "dp", "mp"), P("dp", None, "mp"), P("dp", None, "mp")),
        check_vma=False,
    )
```

```python
import functools

import jax
import jax.numpy as jnp
from jax import lax
from jax.experimental import pallas as pl
from jax.experimental.pallas import tpu as pltpu
from jax.sharding import PartitionSpec as P

VMEM_LIMIT = 48 * 1024 * 1024


def pack_kernel(index_ref, state_ref, base_ref, extra_ref):
    block = pl.program_id(0)
    cap = base_ref.shape[0]
    blocks = pl.num_programs(0)
    for i in range(cap):
        base_ref[i] = state_ref[index_ref[block * cap + i]]

    @pl.when(block == 0)
    def _():
        for i in range(cap):
            extra_ref[i] = state_ref[index_ref[blocks * cap + i]]


def pack(index, state, groups):
    rows, depth, channels = state.shape
    cap = rows // groups
    return pl.pallas_call(
        pack_kernel,
        out_shape=(
            jax.ShapeDtypeStruct((rows, depth, channels), state.dtype),
            jax.ShapeDtypeStruct((cap, depth, channels), state.dtype),
        ),
        grid_spec=pltpu.PrefetchScalarGridSpec(
            num_scalar_prefetch=1,
            grid=(groups,),
            in_specs=[
                pl.BlockSpec((rows, depth, channels), lambda i, _: (0, 0, 0)),
            ],
            out_specs=(
                pl.BlockSpec((cap, depth, channels), lambda i, _: (i, 0, 0)),
                pl.BlockSpec((cap, depth, channels), lambda i, _: (0, 0, 0)),
            ),
        ),
        compiler_params=pltpu.CompilerParams(vmem_limit_bytes=VMEM_LIMIT),
        cost_estimate=pl.CostEstimate(
            flops=0, bytes_accessed=4 * state.size, transcendentals=0
        ),
    )(index, state)


def scan_kernel(
    slot_ref,
    base_ref,
    extra_ref,
    step_ref,
    act_ref,
    gate_ref,
    coef_ref,
    mask_ref,
    decay_ref,
    skip_ref,
    mix_ref,
    final_ref,
    read_ref,
):
    first = pl.program_id(0) * step_ref.shape[1]
    rows_total = base_ref.shape[0]
    steps, rows, channels = step_ref.shape
    width = min(512, channels)

    def one_row(r, carry):
        slot = slot_ref[first + r]
        in_base = slot < rows_total
        at_base = jnp.minimum(slot, rows_total - 1)
        at_extra = jnp.maximum(slot - rows_total, 0)
        coef = coef_ref[r]
        for c in range(0, channels, width):
            cols = pl.ds(c, width)
            hidden = jnp.where(
                in_base,
                base_ref[at_base, :, cols].astype(jnp.float32),
                extra_ref[at_extra, :, cols].astype(jnp.float32),
            )
            decay = decay_ref[:, cols]
            for t in range(steps):
                step = step_ref[t, pl.ds(r, 1), cols]
                act = act_ref[t, pl.ds(r, 1), cols]
                hidden = (
                    jnp.exp(step * decay) * hidden + (step * act) * coef[:, 2 * t : 2 * t + 1]
                )
                read_ref[t, pl.ds(r, 1), cols] = jnp.sum(
                    hidden * coef[:, 2 * t + 1 : 2 * t + 2], axis=0, keepdims=True
                )
            final_ref[r, :, cols] = hidden.astype(final_ref.dtype)
        return carry

    lax.fori_loop(0, rows, one_row, 0)
    for t in range(steps):
        gate = gate_ref[t].astype(jnp.float32)
        mixer = (read_ref[t] + skip_ref[...] * act_ref[t]) * jax.nn.silu(gate)
        mix_ref[t] = jnp.where(mask_ref[:, t : t + 1] > 0, mixer, 0.0).astype(mix_ref.dtype)


def scan(slot, base, extra, step, act, gate, coef, mask, decay, skip):
    rows, depth, channels = base.shape
    steps = step.shape[0]
    tile = 16
    cap = extra.shape[0]

    def whole(shape):
        return pl.BlockSpec(shape, lambda i, _: (0,) * len(shape))

    per_step = pl.BlockSpec((steps, tile, channels), lambda i, _: (0, i, 0))
    return pl.pallas_call(
        scan_kernel,
        out_shape=(
            jax.ShapeDtypeStruct((steps, rows, channels), jnp.bfloat16),
            jax.ShapeDtypeStruct((rows, depth, channels), jnp.bfloat16),
        ),
        grid_spec=pltpu.PrefetchScalarGridSpec(
            num_scalar_prefetch=1,
            grid=(rows // tile,),
            in_specs=[
                whole((rows, depth, channels)),
                whole((cap, depth, channels)),
                per_step,
                per_step,
                per_step,
                pl.BlockSpec((tile, depth, 2 * steps), lambda i, _: (i, 0, 0)),
                pl.BlockSpec((tile, steps), lambda i, _: (i, 0)),
                whole((depth, channels)),
                whole((1, channels)),
            ],
            out_specs=(
                per_step,
                pl.BlockSpec((tile, depth, channels), lambda i, _: (i, 0, 0)),
            ),
            scratch_shapes=[pltpu.VMEM((steps, tile, channels), jnp.float32)],
        ),
        compiler_params=pltpu.CompilerParams(vmem_limit_bytes=VMEM_LIMIT),
        cost_estimate=pl.CostEstimate(
            flops=8 * steps * base.size,
            bytes_accessed=4 * base.size + 16 * step.size,
            transcendentals=steps * base.size,
        ),
    )(slot, base, extra, step, act, gate, coef, mask, decay, skip)


def remote(src, dst, send_sem, recv_sem, peer):
    return pltpu.make_async_remote_copy(
        src_ref=src,
        dst_ref=dst,
        send_sem=send_sem,
        recv_sem=recv_sem,
        device_id={"dp": peer},
        device_id_type=pl.DeviceIdType.MESH,
    )


def move_kernel(
    groups,
    inner,
    from_ref,
    piece_ref,
    conv_ref,
    small_ref,
    ssm_ref,
    out_ref,
    piece_out,
    conv_out,
    small_all,
    ssm_out,
    out_all,
    held,
    passed,
    own_sem,
    send_sem,
    recv_sem,
    gather_send,
    gather_recv,
):
    me = lax.axis_index("dp")
    outer = groups // inner
    mine_z = me // inner
    mine_x = me % inner
    barrier = pltpu.get_barrier_semaphore()
    for k in range(1, groups):
        pl.semaphore_signal(
            barrier,
            inc=1,
            device_id={"dp": (me + k) % groups},
            device_id_type=pl.DeviceIdType.MESH,
        )
    pl.semaphore_wait(barrier, groups - 1)

    def exchange(kind, src, dst):
        copies = []
        for k in range(1, groups):
            peer = (me + k) % groups
            copy = remote(
                src.at[peer], dst.at[me], send_sem.at[kind, k], recv_sem.at[kind, k], peer
            )
            copy.start()
            copies.append(copy)
        own = pltpu.make_async_copy(src.at[me], dst.at[me], own_sem.at[kind])
        own.start()
        return copies, own

    def finish(started):
        copies, own = started
        for copy in copies:
            copy.wait_recv()
        own.wait()

    def gather_copy(kind, src, dst, origin, lane, peer):
        return remote(
            src, dst.at[origin], gather_send.at[kind, origin, lane], gather_recv.at[kind, origin], peer
        )

    def across(kind, src, dst, origin):
        for k in range(1, inner):
            peer = mine_z * inner + (mine_x + k) % inner
            gather_copy(kind, src, dst, origin, 1 + k, peer).start()

    def along(kind, src, dst, origin, up):
        peer = me + inner if up else me - inner
        room = mine_z + 1 < outer if up else mine_z >= 1

        @pl.when(room)
        def _():
            gather_copy(kind, src, dst, origin, 0 if up else 1, peer).start()

    def gather_first(kind, src, dst):
        along(kind, src, dst, me, True)
        along(kind, src, dst, me, False)
        across(kind, src, dst, me)
        own = pltpu.make_async_copy(src, dst.at[me], own_sem.at[kind])
        own.start()
        return own

    def arrived(kind, dst, origin):
        gather_copy(kind, dst.at[origin], dst, origin, 0, me).wait_recv()

    def gather_rest(kind, dst):
        for s in range(1, outer):
            for up in (True, False):
                origin = me - s * inner if up else me + s * inner
                there = mine_z >= s if up else mine_z + s < outer

                @pl.when(there)
                def _():
                    arrived(kind, dst, origin)
                    along(kind, dst.at[origin], dst, origin, up)
                    across(kind, dst.at[origin], dst, origin)

    def gather_end(kind, src, dst, own):
        for z in range(outer):
            for k in range(1, inner):
                arrived(kind, dst, z * inner + (mine_x + k) % inner)
        own.wait()
        for z in range(outer):
            origin = z * inner + mine_x

            @pl.when((mine_z >= z) & (mine_z + 1 < outer))
            def _():
                gather_copy(kind, src, dst, origin, 0, me).wait_send()

            @pl.when((mine_z <= z) & (mine_z >= 1))
            def _():
                gather_copy(kind, src, dst, origin, 1, me).wait_send()

            for k in range(1, inner):
                gather_copy(kind, src, dst, origin, 1 + k, me).wait_send()

    first = exchange(0, piece_ref, held)
    conv = exchange(1, conv_ref, conv_out)
    small_own = gather_first(4, small_ref, small_all)
    ssm = exchange(2, ssm_ref, ssm_out)
    out_own = gather_first(5, out_ref, out_all)
    finish(first)
    for h in range(groups):
        passed[h] = held[from_ref[h]]
    second = exchange(3, passed, piece_out)
    gather_rest(4, small_all)
    gather_rest(5, out_all)
    gather_end(4, small_ref, small_all, small_own)
    finish(conv)
    finish(second)
    gather_end(5, out_ref, out_all, out_own)
    finish(ssm)
    for copies, _ in (first, conv, ssm, second):
        for copy in copies:
            copy.wait_send()


def move(extra_from, pieces, conv, small, ssm, out):
    groups = pieces.shape[0]
    inner = 1
    while inner * inner * 4 <= groups:
        inner *= 2
    held = pl.BlockSpec(memory_space=pl.ANY)

    def like(array):
        return jax.ShapeDtypeStruct(array.shape, array.dtype)

    def gathered(array):
        return jax.ShapeDtypeStruct((groups,) + array.shape, array.dtype)

    return pl.pallas_call(
        functools.partial(move_kernel, groups, inner),
        out_shape=(like(pieces), like(conv), gathered(small), like(ssm), gathered(out)),
        in_specs=[pl.BlockSpec(memory_space=pltpu.SMEM)] + [held] * 5,
        out_specs=(held,) * 5,
        scratch_shapes=[
            pltpu.VMEM(pieces.shape, pieces.dtype),
            pltpu.VMEM(pieces.shape, pieces.dtype),
            pltpu.SemaphoreType.DMA((6,)),
            pltpu.SemaphoreType.DMA((4, groups)),
            pltpu.SemaphoreType.DMA((4, groups)),
            pltpu.SemaphoreType.DMA((6, groups, 1 + inner)),
            pltpu.SemaphoreType.DMA((6, groups)),
        ],
        compiler_params=pltpu.CompilerParams(collective_id=0, has_side_effects=True),
        cost_estimate=pl.CostEstimate(
            flops=0, bytes_accessed=4 * groups * out.size, transcendentals=0
        ),
    )(extra_from, pieces, conv, small, ssm, out)


def mix_kernel(rows_ref, weight_ref, out_ref):
    out_ref[...] = jnp.dot(
        rows_ref[...], weight_ref[0], preferred_element_type=jnp.float32
    ).astype(out_ref.dtype)


def mix(rows, weights):
    groups, channels, width = weights.shape
    count = rows.shape[0]
    return pl.pallas_call(
        mix_kernel,
        out_shape=jax.ShapeDtypeStruct((count, groups * width), jnp.bfloat16),
        grid=(groups,),
        in_specs=[
            pl.BlockSpec((count, channels), lambda g: (0, 0)),
            pl.BlockSpec((1, channels, width), lambda g: (g, 0, 0)),
        ],
        out_specs=pl.BlockSpec((count, width), lambda g: (0, g)),
        compiler_params=pltpu.CompilerParams(vmem_limit_bytes=VMEM_LIMIT),
        cost_estimate=pl.CostEstimate(
            flops=2 * count * weights.size,
            bytes_accessed=2 * weights.size,
            transcendentals=0,
        ),
    )(rows, weights)


def per_device(
    input_steps,
    gate_steps,
    conv_state,
    ssm_state,
    new_slot,
    remaining,
    conv_weight,
    conv_bias,
    coef_proj,
    delta_proj,
    delta_bias,
    decay_log,
    skip_gain,
    out_proj,
):
    groups = lax.axis_size("dp")
    my_group = lax.axis_index("dp")
    row_count, taps_kept, channels = conv_state.shape
    state_len = ssm_state.shape[1]
    steps_total = input_steps.shape[0]
    cap = row_count // groups
    total_rows = new_slot.shape[0]

    target = (new_slot // row_count).reshape(groups, row_count)
    position = jnp.arange(row_count, dtype=jnp.int32)
    earlier = position[None, :] < position[:, None]
    rank = jnp.sum(
        ((target[:, :, None] == target[:, None, :]) & earlier[None]).astype(jnp.int32), axis=2
    )
    source = jnp.broadcast_to(jnp.arange(groups, dtype=jnp.int32)[:, None], rank.shape)
    my_target = lax.dynamic_index_in_dim(target, my_group, 0, keepdims=False)
    my_rank = lax.dynamic_index_in_dim(rank, my_group, 0, keepdims=False)
    leave = jnp.where(
        my_rank < cap, my_target * cap + my_rank, row_count + my_rank - cap
    )
    slots = jnp.arange(row_count + cap, dtype=jnp.int32)
    send_index = jnp.sum(
        jnp.where(slots[:, None] == leave[None, :], position[None, :], 0), axis=1
    )
    arrive = jnp.where(rank < cap, source * cap + rank, row_count + rank - cap)
    here = (new_slot[None, :] == (my_group * row_count + position)[:, None])
    slot = jnp.sum(jnp.where(here, arrive.reshape(1, total_rows), 0), axis=1)
    remain_new = jnp.sum(jnp.where(here, remaining[None, :], 0), axis=1)
    group_ids = jnp.arange(groups, dtype=jnp.int32)
    is_extra = (rank == cap).reshape(1, total_rows)
    extra_from = jnp.sum(
        jnp.where(
            is_extra & (target.reshape(1, total_rows) == group_ids[:, None]),
            source.reshape(1, total_rows),
            0,
        ),
        axis=1,
    )

    def padded(rows, count):
        return jnp.pad(rows, ((0, 0),) * (rows.ndim - 2) + ((0, count - rows.shape[-2]), (0, 0)))

    ssm_base, ssm_extra = pack(send_index, ssm_state, groups)
    conv_packed = conv_state[send_index]
    ssm_rows, conv_rows = cap * state_len, cap * taps_kept
    depth = -(-(ssm_rows + conv_rows) // (16 * groups)) * 16
    extra = jnp.concatenate(
        [
            ssm_extra.reshape(ssm_rows, channels),
            conv_packed[row_count:].reshape(conv_rows, channels),
        ],
        axis=0,
    )
    pieces = padded(extra, groups * depth).reshape(groups, depth, channels)
    conv_depth = -(-conv_rows // 16) * 16
    conv_blocks = padded(
        conv_packed[:row_count].reshape(groups, conv_rows, channels), conv_depth
    )
    coef_width = coef_proj.shape[1]
    coef_depth = -(-coef_width // 16) * 16
    small = jnp.concatenate([padded(coef_proj.T, coef_depth), delta_proj], axis=0)
    extra, conv_base, small, ssm_base, out_whole = move(
        extra_from,
        pieces,
        conv_blocks,
        small,
        ssm_base.reshape(groups, ssm_rows, channels),
        out_proj,
    )
    extra = extra.reshape(groups * depth, channels)
    ssm_base = ssm_base.reshape(row_count, state_len, channels)
    ssm_extra = extra[:ssm_rows].reshape(cap, state_len, channels)
    conv_extra = extra[ssm_rows : ssm_rows + conv_rows].reshape(cap, taps_kept, channels)
    conv_base = conv_base[:, :conv_rows].reshape(row_count, taps_kept, channels)
    coef_whole = small[:, :coef_width].reshape(groups * coef_width, channels)
    delta_whole = small[:, coef_depth:].reshape(-1, channels)
    rank_len = delta_whole.shape[0]

    conv_moved = jnp.concatenate([conv_base, conv_extra], axis=0)[slot]
    sequence = [conv_moved[:, k] for k in range(taps_kept)]
    sequence += [input_steps[t] for t in range(steps_total)]
    wide = [entry.astype(jnp.float32) for entry in sequence]
    activated = jnp.stack(
        [
            jax.nn.silu(
                sum(wide[t + k] * conv_weight[k][None] for k in range(taps_kept + 1)) + conv_bias
            )
            for t in range(steps_total)
        ]
    )
    partial_value = lax.dot_general(
        activated.reshape(steps_total * row_count, channels).astype(jnp.bfloat16),
        coef_whole,
        (((1,), (1,)), ((), ())),
        preferred_element_type=jnp.float32,
    )
    low_rank = lax.psum(partial_value.astype(jnp.bfloat16), "mp")
    coef = low_rank[:, rank_len:].astype(jnp.float32)
    coef = coef.reshape(steps_total, row_count, 2, state_len)
    coef = coef.transpose(1, 3, 0, 2).reshape(row_count, state_len, 2 * steps_total)
    active = remain_new[:, None] > jnp.arange(steps_total, dtype=jnp.int32)[None, :]
    step_size = jax.nn.softplus(
        jnp.dot(low_rank[:, :rank_len], delta_whole, preferred_element_type=jnp.float32)
        + delta_bias
    ).reshape(steps_total, row_count, channels)
    step_size = jnp.where(active.T[:, :, None], step_size, 0.0)

    mixed, ssm_final = scan(
        slot,
        ssm_base,
        ssm_extra,
        step_size,
        activated,
        gate_steps,
        coef,
        active.astype(jnp.int32),
        -jnp.exp(decay_log),
        skip_gain[None],
    )
    last = jnp.minimum(remain_new, steps_total)[:, None]
    window = []
    for k in range(taps_kept):
        entry = sequence[k]
        for t in range(1, steps_total + 1):
            entry = jnp.where(last == t, sequence[k + t], entry)
        window.append(entry)
    conv_final = jnp.stack(window, axis=1)

    partial_mix = mix(mixed.reshape(steps_total * row_count, channels), out_whole)
    summed = lax.psum_scatter(
        partial_mix, "mp", scatter_dimension=1, tiled=True
    )
    layer_out = summed.reshape(steps_total, row_count, summed.shape[1])
    return (layer_out, conv_final, ssm_final)


def solution(mesh):
    return jax.shard_map(
        per_device,
        mesh=mesh,
        in_specs=(
            P(None, "dp", "mp"),
            P(None, "dp", "mp"),
            P("dp", None, "mp"),
            P("dp", None, "mp"),
            P(),
            P(),
            P(None, "mp"),
            P("mp"),
            P("mp", "dp"),
            P("dp", "mp"),
            P("mp"),
            P(None, "mp"),
            P("mp"),
            P("mp", "dp"),
        ),
        out_specs=(P(None, "dp", "mp"), P("dp", None, "mp"), P("dp", None, "mp")),
        check_vma=False,
    )
```

```python
import functools

import jax
import jax.numpy as jnp
from jax import lax
from jax.experimental import pallas as pl
from jax.experimental.pallas import tpu as pltpu
from jax.sharding import PartitionSpec as P

VMEM_LIMIT = 48 * 1024 * 1024
CHUNKS = 4


def pack_kernel(index_ref, state_ref, base_ref, extra_ref):
    block = pl.program_id(0)
    cap = base_ref.shape[0]
    blocks = pl.num_programs(0)
    for i in range(cap):
        base_ref[i] = state_ref[index_ref[block * cap + i]]

    @pl.when(block == 0)
    def _():
        for i in range(cap):
            extra_ref[i] = state_ref[index_ref[blocks * cap + i]]


def pack(index, state, groups):
    rows, depth, channels = state.shape
    cap = rows // groups
    return pl.pallas_call(
        pack_kernel,
        out_shape=(
            jax.ShapeDtypeStruct((rows, depth, channels), state.dtype),
            jax.ShapeDtypeStruct((cap, depth, channels), state.dtype),
        ),
        grid_spec=pltpu.PrefetchScalarGridSpec(
            num_scalar_prefetch=1,
            grid=(groups,),
            in_specs=[
                pl.BlockSpec((rows, depth, channels), lambda i, _: (0, 0, 0)),
            ],
            out_specs=(
                pl.BlockSpec((cap, depth, channels), lambda i, _: (i, 0, 0)),
                pl.BlockSpec((cap, depth, channels), lambda i, _: (0, 0, 0)),
            ),
        ),
        compiler_params=pltpu.CompilerParams(vmem_limit_bytes=VMEM_LIMIT),
        cost_estimate=pl.CostEstimate(
            flops=0, bytes_accessed=4 * state.size, transcendentals=0
        ),
    )(index, state)


def scan_kernel(
    start,
    slot_ref,
    base_ref,
    extra_ref,
    step_ref,
    act_ref,
    gate_ref,
    coef_ref,
    mask_ref,
    decay_ref,
    skip_ref,
    mix_ref,
    final_ref,
    read_ref,
):
    first = (start + pl.program_id(0)) * step_ref.shape[1]
    rows_total = base_ref.shape[0]
    steps, rows, channels = step_ref.shape
    width = min(512, channels)

    def one_row(r, carry):
        slot = slot_ref[first + r]
        in_base = slot < rows_total
        at_base = jnp.minimum(slot, rows_total - 1)
        at_extra = jnp.maximum(slot - rows_total, 0)
        coef = coef_ref[r]
        for c in range(0, channels, width):
            cols = pl.ds(c, width)
            hidden = jnp.where(
                in_base,
                base_ref[at_base, :, cols].astype(jnp.float32),
                extra_ref[at_extra, :, cols].astype(jnp.float32),
            )
            decay = decay_ref[:, cols]
            for t in range(steps):
                step = step_ref[t, pl.ds(r, 1), cols]
                act = act_ref[t, pl.ds(r, 1), cols]
                hidden = (
                    jnp.exp(step * decay) * hidden + (step * act) * coef[:, 2 * t : 2 * t + 1]
                )
                read_ref[t, pl.ds(r, 1), cols] = jnp.sum(
                    hidden * coef[:, 2 * t + 1 : 2 * t + 2], axis=0, keepdims=True
                )
            final_ref[r, :, cols] = hidden.astype(final_ref.dtype)
        return carry

    lax.fori_loop(0, rows, one_row, 0)
    for t in range(steps):
        gate = gate_ref[t].astype(jnp.float32)
        mixer = (read_ref[t] + skip_ref[...] * act_ref[t]) * jax.nn.silu(gate)
        mix_ref[t] = jnp.where(mask_ref[:, t : t + 1] > 0, mixer, 0.0).astype(mix_ref.dtype)


def scan(part, parts, slot, base, extra, step, act, gate, coef, mask, decay, skip):
    rows, depth, channels = base.shape
    steps = step.shape[0]
    tile = 16
    count = rows // parts
    start = part * count // tile
    cap = extra.shape[0]

    def whole(shape):
        return pl.BlockSpec(shape, lambda i, _: (0,) * len(shape))

    per_step = pl.BlockSpec((steps, tile, channels), lambda i, _: (0, start + i, 0))
    return pl.pallas_call(
        functools.partial(scan_kernel, start),
        out_shape=(
            jax.ShapeDtypeStruct((steps, count, channels), jnp.bfloat16),
            jax.ShapeDtypeStruct((count, depth, channels), jnp.bfloat16),
        ),
        grid_spec=pltpu.PrefetchScalarGridSpec(
            num_scalar_prefetch=1,
            grid=(count // tile,),
            in_specs=[
                whole((rows, depth, channels)),
                whole((cap, depth, channels)),
                per_step,
                per_step,
                per_step,
                pl.BlockSpec((tile, depth, 2 * steps), lambda i, _: (start + i, 0, 0)),
                pl.BlockSpec((tile, steps), lambda i, _: (start + i, 0)),
                whole((depth, channels)),
                whole((1, channels)),
            ],
            out_specs=(
                pl.BlockSpec((steps, tile, channels), lambda i, _: (0, i, 0)),
                pl.BlockSpec((tile, depth, channels), lambda i, _: (i, 0, 0)),
            ),
            scratch_shapes=[pltpu.VMEM((steps, tile, channels), jnp.float32)],
        ),
        compiler_params=pltpu.CompilerParams(vmem_limit_bytes=VMEM_LIMIT),
        cost_estimate=pl.CostEstimate(
            flops=8 * steps * base.size // parts,
            bytes_accessed=4 * base.size + 16 * step.size,
            transcendentals=steps * base.size // parts,
        ),
    )(slot, base, extra, step, act, gate, coef, mask, decay, skip)


def remote(src, dst, send_sem, recv_sem, peer):
    return pltpu.make_async_remote_copy(
        src_ref=src,
        dst_ref=dst,
        send_sem=send_sem,
        recv_sem=recv_sem,
        device_id={"dp": peer},
        device_id_type=pl.DeviceIdType.MESH,
    )


def move_kernel(
    groups,
    inner,
    from_ref,
    piece_ref,
    conv_ref,
    small_ref,
    out_ref,
    piece_out,
    conv_out,
    small_all,
    out_all,
    held,
    passed,
    own_sem,
    send_sem,
    recv_sem,
    gather_send,
    gather_recv,
):
    me = lax.axis_index("dp")
    outer = groups // inner
    mine_z = me // inner
    mine_x = me % inner
    barrier = pltpu.get_barrier_semaphore()
    for k in range(1, groups):
        pl.semaphore_signal(
            barrier,
            inc=1,
            device_id={"dp": (me + k) % groups},
            device_id_type=pl.DeviceIdType.MESH,
        )
    pl.semaphore_wait(barrier, groups - 1)

    def exchange(kind, src, dst):
        copies = []
        for k in range(1, groups):
            peer = (me + k) % groups
            copy = remote(
                src.at[peer], dst.at[me], send_sem.at[kind, k], recv_sem.at[kind, k], peer
            )
            copy.start()
            copies.append(copy)
        own = pltpu.make_async_copy(src.at[me], dst.at[me], own_sem.at[CHUNKS + 1 + kind])
        own.start()
        return copies, own

    def finish(started):
        copies, own = started
        for copy in copies:
            copy.wait_recv()
        own.wait()

    def gather_copy(kind, src, dst, origin, lane, peer):
        return remote(
            src, dst.at[origin], gather_send.at[kind, origin, lane], gather_recv.at[kind, origin], peer
        )

    def across(kind, src, dst, origin):
        for k in range(1, inner):
            peer = mine_z * inner + (mine_x + k) % inner
            gather_copy(kind, src, dst, origin, 1 + k, peer).start()

    def along(kind, src, dst, origin, up):
        peer = me + inner if up else me - inner
        room = mine_z + 1 < outer if up else mine_z >= 1

        @pl.when(room)
        def _():
            gather_copy(kind, src, dst, origin, 0 if up else 1, peer).start()

    def gather_first(kind, src, dst):
        along(kind, src, dst, me, True)
        along(kind, src, dst, me, False)
        across(kind, src, dst, me)
        own = pltpu.make_async_copy(src, dst.at[me], own_sem.at[kind])
        own.start()
        return own

    def arrived(kind, dst, origin):
        gather_copy(kind, dst.at[origin], dst, origin, 0, me).wait_recv()

    def gather_rest(kind, dst, s):
        for up in (True, False):
            origin = me - s * inner if up else me + s * inner
            there = mine_z >= s if up else mine_z + s < outer

            @pl.when(there)
            def _():
                arrived(kind, dst, origin)
                along(kind, dst.at[origin], dst, origin, up)
                across(kind, dst.at[origin], dst, origin)

    def gather_end(kind, src, dst, own):
        for z in range(outer):
            for k in range(1, inner):
                arrived(kind, dst, z * inner + (mine_x + k) % inner)
        own.wait()
        for z in range(outer):
            origin = z * inner + mine_x

            @pl.when((mine_z >= z) & (mine_z + 1 < outer))
            def _():
                gather_copy(kind, src, dst, origin, 0, me).wait_send()

            @pl.when((mine_z <= z) & (mine_z >= 1))
            def _():
                gather_copy(kind, src, dst, origin, 1, me).wait_send()

            for k in range(1, inner):
                gather_copy(kind, src, dst, origin, 1 + k, me).wait_send()

    first = exchange(0, piece_ref, held)
    conv = exchange(1, conv_ref, conv_out)
    small_own = gather_first(CHUNKS, small_ref, small_all)
    depth = out_ref.shape[0] // CHUNKS
    parts = [
        (c, out_ref.at[pl.ds(c * depth, depth)], out_all.at[:, pl.ds(c * depth, depth)])
        for c in range(CHUNKS)
    ]
    out_own = [gather_first(*part) for part in parts]
    finish(first)
    for h in range(groups):
        passed[h] = held[from_ref[h]]
    second = exchange(2, passed, piece_out)
    for s in range(1, outer):
        gather_rest(CHUNKS, small_all, s)
        for c, _, whole in parts:
            gather_rest(c, whole, s)
    gather_end(CHUNKS, small_ref, small_all, small_own)
    finish(conv)
    finish(second)
    for (c, part, whole), own in zip(parts, out_own):
        gather_end(c, part, whole, own)
    for copies, _ in (first, conv, second):
        for copy in copies:
            copy.wait_send()


def move(extra_from, pieces, conv, small, out):
    groups = pieces.shape[0]
    inner = 1
    while inner * inner * 4 <= groups:
        inner *= 2
    held = pl.BlockSpec(memory_space=pl.ANY)

    def like(array):
        return jax.ShapeDtypeStruct(array.shape, array.dtype)

    def gathered(array):
        return jax.ShapeDtypeStruct((groups,) + array.shape, array.dtype)

    return pl.pallas_call(
        functools.partial(move_kernel, groups, inner),
        out_shape=(like(pieces), like(conv), gathered(small), gathered(out)),
        in_specs=[pl.BlockSpec(memory_space=pltpu.SMEM)] + [held] * 4,
        out_specs=(held,) * 4,
        scratch_shapes=[
            pltpu.VMEM(pieces.shape, pieces.dtype),
            pltpu.VMEM(pieces.shape, pieces.dtype),
            pltpu.SemaphoreType.DMA((CHUNKS + 4,)),
            pltpu.SemaphoreType.DMA((3, groups)),
            pltpu.SemaphoreType.DMA((3, groups)),
            pltpu.SemaphoreType.DMA((CHUNKS + 1, groups, 1 + inner)),
            pltpu.SemaphoreType.DMA((CHUNKS + 1, groups)),
        ],
        compiler_params=pltpu.CompilerParams(collective_id=0, has_side_effects=True),
        cost_estimate=pl.CostEstimate(
            flops=0, bytes_accessed=4 * groups * out.size, transcendentals=0
        ),
    )(extra_from, pieces, conv, small, out)


def mix_kernel(rows_ref, weight_ref, out_ref):
    out_ref[...] = jnp.dot(
        rows_ref[...], weight_ref[0], preferred_element_type=jnp.float32
    ).astype(out_ref.dtype)


def mix(rows, weights):
    groups, channels, width = weights.shape
    count = rows.shape[0]
    return pl.pallas_call(
        mix_kernel,
        out_shape=jax.ShapeDtypeStruct((count, groups * width), jnp.bfloat16),
        grid=(groups,),
        in_specs=[
            pl.BlockSpec((count, channels), lambda g: (0, 0)),
            pl.BlockSpec((1, channels, width), lambda g: (g, 0, 0)),
        ],
        out_specs=pl.BlockSpec((count, width), lambda g: (0, g)),
        compiler_params=pltpu.CompilerParams(vmem_limit_bytes=VMEM_LIMIT),
        cost_estimate=pl.CostEstimate(
            flops=2 * count * weights.size,
            bytes_accessed=2 * weights.size,
            transcendentals=0,
        ),
    )(rows, weights)


def per_device(
    input_steps,
    gate_steps,
    conv_state,
    ssm_state,
    new_slot,
    remaining,
    conv_weight,
    conv_bias,
    coef_proj,
    delta_proj,
    delta_bias,
    decay_log,
    skip_gain,
    out_proj,
):
    groups = lax.axis_size("dp")
    my_group = lax.axis_index("dp")
    row_count, taps_kept, channels = conv_state.shape
    state_len = ssm_state.shape[1]
    steps_total = input_steps.shape[0]
    cap = row_count // groups
    total_rows = new_slot.shape[0]

    target = (new_slot // row_count).reshape(groups, row_count)
    position = jnp.arange(row_count, dtype=jnp.int32)
    earlier = position[None, :] < position[:, None]
    rank = jnp.sum(
        ((target[:, :, None] == target[:, None, :]) & earlier[None]).astype(jnp.int32), axis=2
    )
    source = jnp.broadcast_to(jnp.arange(groups, dtype=jnp.int32)[:, None], rank.shape)
    my_target = lax.dynamic_index_in_dim(target, my_group, 0, keepdims=False)
    my_rank = lax.dynamic_index_in_dim(rank, my_group, 0, keepdims=False)
    leave = jnp.where(
        my_rank < cap, my_target * cap + my_rank, row_count + my_rank - cap
    )
    slots = jnp.arange(row_count + cap, dtype=jnp.int32)
    send_index = jnp.sum(
        jnp.where(slots[:, None] == leave[None, :], position[None, :], 0), axis=1
    )
    arrive = jnp.where(rank < cap, source * cap + rank, row_count + rank - cap)
    here = (new_slot[None, :] == (my_group * row_count + position)[:, None])
    slot = jnp.sum(jnp.where(here, arrive.reshape(1, total_rows), 0), axis=1)
    remain_new = jnp.sum(jnp.where(here, remaining[None, :], 0), axis=1)
    group_ids = jnp.arange(groups, dtype=jnp.int32)
    is_extra = (rank == cap).reshape(1, total_rows)
    extra_from = jnp.sum(
        jnp.where(
            is_extra & (target.reshape(1, total_rows) == group_ids[:, None]),
            source.reshape(1, total_rows),
            0,
        ),
        axis=1,
    )

    def padded(rows, count):
        return jnp.pad(rows, ((0, 0),) * (rows.ndim - 2) + ((0, count - rows.shape[-2]), (0, 0)))

    ssm_base, ssm_extra = pack(send_index, ssm_state, groups)
    conv_packed = conv_state[send_index]
    ssm_rows, conv_rows = cap * state_len, cap * taps_kept
    depth = -(-(ssm_rows + conv_rows) // (16 * groups)) * 16
    extra = jnp.concatenate(
        [
            ssm_extra.reshape(ssm_rows, channels),
            conv_packed[row_count:].reshape(conv_rows, channels),
        ],
        axis=0,
    )
    pieces = padded(extra, groups * depth).reshape(groups, depth, channels)
    conv_depth = -(-conv_rows // 16) * 16
    conv_blocks = padded(
        conv_packed[:row_count].reshape(groups, conv_rows, channels), conv_depth
    )
    coef_width = coef_proj.shape[1]
    coef_depth = -(-coef_width // 16) * 16
    small = jnp.concatenate([padded(coef_proj.T, coef_depth), delta_proj], axis=0)
    ssm_base = lax.all_to_all(ssm_base, "dp", split_axis=0, concat_axis=0, tiled=True)
    extra, conv_base, small, out_whole = move(
        extra_from,
        pieces,
        conv_blocks,
        small,
        out_proj,
    )
    extra = extra.reshape(groups * depth, channels)
    ssm_extra = extra[:ssm_rows].reshape(cap, state_len, channels)
    conv_extra = extra[ssm_rows : ssm_rows + conv_rows].reshape(cap, taps_kept, channels)
    conv_base = conv_base[:, :conv_rows].reshape(row_count, taps_kept, channels)
    coef_whole = small[:, :coef_width].reshape(groups * coef_width, channels)
    delta_whole = small[:, coef_depth:].reshape(-1, channels)
    rank_len = delta_whole.shape[0]

    conv_moved = jnp.concatenate([conv_base, conv_extra], axis=0)[slot]
    sequence = [conv_moved[:, k] for k in range(taps_kept)]
    sequence += [input_steps[t] for t in range(steps_total)]
    wide = [entry.astype(jnp.float32) for entry in sequence]
    activated = jnp.stack(
        [
            jax.nn.silu(
                sum(wide[t + k] * conv_weight[k][None] for k in range(taps_kept + 1)) + conv_bias
            )
            for t in range(steps_total)
        ]
    )
    partial_value = lax.dot_general(
        activated.reshape(steps_total * row_count, channels).astype(jnp.bfloat16),
        coef_whole,
        (((1,), (1,)), ((), ())),
        preferred_element_type=jnp.float32,
    )
    low_rank = lax.psum(partial_value.astype(jnp.bfloat16), "mp")
    coef = low_rank[:, rank_len:].astype(jnp.float32)
    coef = coef.reshape(steps_total, row_count, 2, state_len)
    coef = coef.transpose(1, 3, 0, 2).reshape(row_count, state_len, 2 * steps_total)
    active = remain_new[:, None] > jnp.arange(steps_total, dtype=jnp.int32)[None, :]
    step_size = jax.nn.softplus(
        jnp.dot(low_rank[:, :rank_len], delta_whole, preferred_element_type=jnp.float32)
        + delta_bias
    ).reshape(steps_total, row_count, channels)
    step_size = jnp.where(active.T[:, :, None], step_size, 0.0)

    decay_rate = -jnp.exp(decay_log)
    parts = 2
    layer_parts, final_parts = [], []
    for part in range(parts):
        mixed, final = scan(
            part,
            parts,
            slot,
            ssm_base,
            ssm_extra,
            step_size,
            activated,
            gate_steps,
            coef,
            active.astype(jnp.int32),
            decay_rate,
            skip_gain[None],
        )
        partial_mix = mix(mixed.reshape(-1, channels), out_whole)
        summed = lax.psum_scatter(partial_mix, "mp", scatter_dimension=1, tiled=True)
        layer_parts.append(summed.reshape(steps_total, row_count // parts, -1))
        final_parts.append(final)
    layer_out = jnp.concatenate(layer_parts, axis=1)
    ssm_final = jnp.concatenate(final_parts, axis=0)
    last = jnp.minimum(remain_new, steps_total)[:, None]
    window = []
    for k in range(taps_kept):
        entry = sequence[k]
        for t in range(1, steps_total + 1):
            entry = jnp.where(last == t, sequence[k + t], entry)
        window.append(entry)
    conv_final = jnp.stack(window, axis=1)
    return (layer_out, conv_final, ssm_final)


def solution(mesh):
    return jax.shard_map(
        per_device,
        mesh=mesh,
        in_specs=(
            P(None, "dp", "mp"),
            P(None, "dp", "mp"),
            P("dp", None, "mp"),
            P("dp", None, "mp"),
            P(),
            P(),
            P(None, "mp"),
            P("mp"),
            P("mp", "dp"),
            P("dp", "mp"),
            P("mp"),
            P(None, "mp"),
            P("mp"),
            P("mp", "dp"),
        ),
        out_specs=(P(None, "dp", "mp"), P("dp", None, "mp"), P("dp", None, "mp")),
        check_vma=False,
    )
```

```python
import functools

import jax
import jax.numpy as jnp
from jax import lax
from jax.experimental import pallas as pl
from jax.experimental.pallas import tpu as pltpu
from jax.sharding import PartitionSpec as P

VMEM_LIMIT = 48 * 1024 * 1024
CHUNKS = 4


def pack_kernel(index_ref, state_ref, base_ref, extra_ref):
    block = pl.program_id(0)
    cap = base_ref.shape[0]
    blocks = pl.num_programs(0)
    for i in range(cap):
        base_ref[i] = state_ref[index_ref[block * cap + i]]

    @pl.when(block == 0)
    def _():
        for i in range(cap):
            extra_ref[i] = state_ref[index_ref[blocks * cap + i]]


def pack(index, state, groups):
    rows, depth, channels = state.shape
    cap = rows // groups
    return pl.pallas_call(
        pack_kernel,
        out_shape=(
            jax.ShapeDtypeStruct((rows, depth, channels), state.dtype),
            jax.ShapeDtypeStruct((cap, depth, channels), state.dtype),
        ),
        grid_spec=pltpu.PrefetchScalarGridSpec(
            num_scalar_prefetch=1,
            grid=(groups,),
            in_specs=[
                pl.BlockSpec((rows, depth, channels), lambda i, _: (0, 0, 0)),
            ],
            out_specs=(
                pl.BlockSpec((cap, depth, channels), lambda i, _: (i, 0, 0)),
                pl.BlockSpec((cap, depth, channels), lambda i, _: (0, 0, 0)),
            ),
        ),
        compiler_params=pltpu.CompilerParams(vmem_limit_bytes=VMEM_LIMIT),
        cost_estimate=pl.CostEstimate(
            flops=0, bytes_accessed=4 * state.size, transcendentals=0
        ),
    )(index, state)


def scan_kernel(
    start,
    slot_ref,
    base_ref,
    extra_ref,
    step_ref,
    act_ref,
    gate_ref,
    coef_ref,
    mask_ref,
    decay_ref,
    skip_ref,
    mix_ref,
    final_ref,
    read_ref,
):
    first = (start + pl.program_id(0)) * step_ref.shape[1]
    rows_total = base_ref.shape[0]
    steps, rows, channels = step_ref.shape
    width = min(512, channels)

    def one_row(r, carry):
        slot = slot_ref[first + r]
        in_base = slot < rows_total
        at_base = jnp.minimum(slot, rows_total - 1)
        at_extra = jnp.maximum(slot - rows_total, 0)
        coef = coef_ref[r]
        for c in range(0, channels, width):
            cols = pl.ds(c, width)
            hidden = jnp.where(
                in_base,
                base_ref[at_base, :, cols].astype(jnp.float32),
                extra_ref[at_extra, :, cols].astype(jnp.float32),
            )
            decay = decay_ref[:, cols]
            for t in range(steps):
                step = step_ref[t, pl.ds(r, 1), cols]
                act = act_ref[t, pl.ds(r, 1), cols]
                hidden = (
                    jnp.exp(step * decay) * hidden + (step * act) * coef[:, 2 * t : 2 * t + 1]
                )
                read_ref[t, pl.ds(r, 1), cols] = jnp.sum(
                    hidden * coef[:, 2 * t + 1 : 2 * t + 2], axis=0, keepdims=True
                )
            final_ref[r, :, cols] = hidden.astype(final_ref.dtype)
        return carry

    lax.fori_loop(0, rows, one_row, 0)
    for t in range(steps):
        gate = gate_ref[t].astype(jnp.float32)
        mixer = (read_ref[t] + skip_ref[...] * act_ref[t]) * jax.nn.silu(gate)
        mix_ref[t] = jnp.where(mask_ref[:, t : t + 1] > 0, mixer, 0.0).astype(mix_ref.dtype)


def scan(part, parts, slot, base, extra, step, act, gate, coef, mask, decay, skip):
    rows, depth, channels = base.shape
    steps = step.shape[0]
    tile = 16
    count = rows // parts
    start = part * count // tile
    cap = extra.shape[0]

    def whole(shape):
        return pl.BlockSpec(shape, lambda i, _: (0,) * len(shape))

    per_step = pl.BlockSpec((steps, tile, channels), lambda i, _: (0, start + i, 0))
    return pl.pallas_call(
        functools.partial(scan_kernel, start),
        out_shape=(
            jax.ShapeDtypeStruct((steps, count, channels), jnp.bfloat16),
            jax.ShapeDtypeStruct((count, depth, channels), jnp.bfloat16),
        ),
        grid_spec=pltpu.PrefetchScalarGridSpec(
            num_scalar_prefetch=1,
            grid=(count // tile,),
            in_specs=[
                whole((rows, depth, channels)),
                whole((cap, depth, channels)),
                per_step,
                per_step,
                per_step,
                pl.BlockSpec((tile, depth, 2 * steps), lambda i, _: (start + i, 0, 0)),
                pl.BlockSpec((tile, steps), lambda i, _: (start + i, 0)),
                whole((depth, channels)),
                whole((1, channels)),
            ],
            out_specs=(
                pl.BlockSpec((steps, tile, channels), lambda i, _: (0, i, 0)),
                pl.BlockSpec((tile, depth, channels), lambda i, _: (i, 0, 0)),
            ),
            scratch_shapes=[pltpu.VMEM((steps, tile, channels), jnp.float32)],
        ),
        compiler_params=pltpu.CompilerParams(vmem_limit_bytes=VMEM_LIMIT),
        cost_estimate=pl.CostEstimate(
            flops=8 * steps * base.size // parts,
            bytes_accessed=4 * base.size + 16 * step.size,
            transcendentals=steps * base.size // parts,
        ),
    )(slot, base, extra, step, act, gate, coef, mask, decay, skip)


def remote(src, dst, send_sem, recv_sem, peer):
    return pltpu.make_async_remote_copy(
        src_ref=src,
        dst_ref=dst,
        send_sem=send_sem,
        recv_sem=recv_sem,
        device_id={"dp": peer},
        device_id_type=pl.DeviceIdType.MESH,
    )


def greet(groups):
    me = lax.axis_index("dp")
    barrier = pltpu.get_barrier_semaphore()
    for k in range(1, groups):
        pl.semaphore_signal(
            barrier,
            inc=1,
            device_id={"dp": (me + k) % groups},
            device_id_type=pl.DeviceIdType.MESH,
        )
    pl.semaphore_wait(barrier, groups - 1)


def gather_blocks(groups, inner, parts, own_sem, send_sem, recv_sem, between):
    me = lax.axis_index("dp")
    outer = groups // inner
    mine_z = me // inner
    mine_x = me % inner

    def copy_of(kind, src, dst, origin, lane, peer):
        return remote(
            src, dst.at[origin], send_sem.at[kind, origin, lane], recv_sem.at[kind, origin], peer
        )

    def forward(kind, src, dst, origin, ups):
        for up in ups:
            peer = me + inner if up else me - inner
            room = mine_z + 1 < outer if up else mine_z >= 1

            @pl.when(room)
            def _():
                copy_of(kind, src, dst, origin, 0 if up else 1, peer).start()

        for k in range(1, inner):
            peer = mine_z * inner + (mine_x + k) % inner
            copy_of(kind, src, dst, origin, 1 + k, peer).start()

    def arrived(kind, dst, origin):
        copy_of(kind, dst.at[origin], dst, origin, 0, me).wait_recv()

    own = []
    for kind, (src, dst) in enumerate(parts):
        forward(kind, src, dst, me, (True, False))
        copy = pltpu.make_async_copy(src, dst.at[me], own_sem.at[kind])
        copy.start()
        own.append(copy)
    between()
    for s in range(1, outer):
        for kind, (_, dst) in enumerate(parts):
            for up in (True, False):
                origin = me - s * inner if up else me + s * inner
                there = mine_z >= s if up else mine_z + s < outer

                @pl.when(there)
                def _():
                    arrived(kind, dst, origin)
                    forward(kind, dst.at[origin], dst, origin, (up,))

    for kind, (src, dst) in enumerate(parts):
        for z in range(outer):
            for k in range(1, inner):
                arrived(kind, dst, z * inner + (mine_x + k) % inner)
        own[kind].wait()
        for z in range(outer):
            origin = z * inner + mine_x

            @pl.when((mine_z >= z) & (mine_z + 1 < outer))
            def _():
                copy_of(kind, src, dst, origin, 0, me).wait_send()

            @pl.when((mine_z <= z) & (mine_z >= 1))
            def _():
                copy_of(kind, src, dst, origin, 1, me).wait_send()

            for k in range(1, inner):
                copy_of(kind, src, dst, origin, 1 + k, me).wait_send()


def move_kernel(
    groups,
    inner,
    from_ref,
    piece_ref,
    conv_ref,
    small_ref,
    piece_out,
    conv_out,
    small_all,
    held,
    passed,
    own_sem,
    send_sem,
    recv_sem,
    gather_own,
    gather_send,
    gather_recv,
):
    me = lax.axis_index("dp")
    greet(groups)

    def exchange(kind, src, dst):
        copies = []
        for k in range(1, groups):
            peer = (me + k) % groups
            copy = remote(
                src.at[peer], dst.at[me], send_sem.at[kind, k], recv_sem.at[kind, k], peer
            )
            copy.start()
            copies.append(copy)
        own = pltpu.make_async_copy(src.at[me], dst.at[me], own_sem.at[kind])
        own.start()
        return copies, own

    def finish(started):
        copies, own = started
        for copy in copies:
            copy.wait_recv()
        own.wait()

    first = exchange(0, piece_ref, held)
    conv = exchange(1, conv_ref, conv_out)
    second = []

    def pass_on():
        finish(first)
        for h in range(groups):
            passed[h] = held[from_ref[h]]
        second.append(exchange(2, passed, piece_out))

    gather_blocks(
        groups, inner, [(small_ref, small_all)], gather_own, gather_send, gather_recv, pass_on
    )
    finish(conv)
    finish(second[0])
    for copies, _ in (first, conv, second[0]):
        for copy in copies:
            copy.wait_send()


def gather_kernel(groups, inner, src_ref, all_ref, own_sem, send_sem, recv_sem):
    greet(groups)
    depth = src_ref.shape[0] // CHUNKS
    parts = [
        (src_ref.at[pl.ds(c * depth, depth)], all_ref.at[:, pl.ds(c * depth, depth)])
        for c in range(CHUNKS)
    ]
    gather_blocks(groups, inner, parts, own_sem, send_sem, recv_sem, lambda: None)


def inner_of(groups):
    inner = 1
    while inner * inner * 4 <= groups:
        inner *= 2
    return inner


def gather_scratch(kinds, groups, inner):
    return [
        pltpu.SemaphoreType.DMA((kinds,)),
        pltpu.SemaphoreType.DMA((kinds, groups, 1 + inner)),
        pltpu.SemaphoreType.DMA((kinds, groups)),
    ]


def move(extra_from, pieces, conv, small):
    groups = pieces.shape[0]
    inner = inner_of(groups)
    held = pl.BlockSpec(memory_space=pl.ANY)

    def like(array):
        return jax.ShapeDtypeStruct(array.shape, array.dtype)

    return pl.pallas_call(
        functools.partial(move_kernel, groups, inner),
        out_shape=(
            like(pieces),
            like(conv),
            jax.ShapeDtypeStruct((groups,) + small.shape, small.dtype),
        ),
        in_specs=[pl.BlockSpec(memory_space=pltpu.SMEM)] + [held] * 3,
        out_specs=(held,) * 3,
        scratch_shapes=[
            pltpu.VMEM(pieces.shape, pieces.dtype),
            pltpu.VMEM(pieces.shape, pieces.dtype),
            pltpu.SemaphoreType.DMA((3,)),
            pltpu.SemaphoreType.DMA((3, groups)),
            pltpu.SemaphoreType.DMA((3, groups)),
        ]
        + gather_scratch(1, groups, inner),
        compiler_params=pltpu.CompilerParams(collective_id=0, has_side_effects=True),
        cost_estimate=pl.CostEstimate(
            flops=0, bytes_accessed=64 * groups * small.size, transcendentals=0
        ),
    )(extra_from, pieces, conv, small)


def gather(block, groups):
    inner = inner_of(groups)
    held = pl.BlockSpec(memory_space=pl.ANY)
    return pl.pallas_call(
        functools.partial(gather_kernel, groups, inner),
        out_shape=jax.ShapeDtypeStruct((groups,) + block.shape, block.dtype),
        in_specs=[held],
        out_specs=held,
        scratch_shapes=gather_scratch(CHUNKS, groups, inner),
        compiler_params=pltpu.CompilerParams(collective_id=1, has_side_effects=True),
        cost_estimate=pl.CostEstimate(
            flops=0, bytes_accessed=32 * groups * block.size, transcendentals=0
        ),
    )(block)


def mix_kernel(rows_ref, weight_ref, out_ref):
    out_ref[...] = jnp.dot(
        rows_ref[...], weight_ref[0], preferred_element_type=jnp.float32
    ).astype(out_ref.dtype)


def mix(rows, weights):
    groups, channels, width = weights.shape
    count = rows.shape[0]
    return pl.pallas_call(
        mix_kernel,
        out_shape=jax.ShapeDtypeStruct((count, groups * width), jnp.bfloat16),
        grid=(groups,),
        in_specs=[
            pl.BlockSpec((count, channels), lambda g: (0, 0)),
            pl.BlockSpec((1, channels, width), lambda g: (g, 0, 0)),
        ],
        out_specs=pl.BlockSpec((count, width), lambda g: (0, g)),
        compiler_params=pltpu.CompilerParams(vmem_limit_bytes=VMEM_LIMIT),
        cost_estimate=pl.CostEstimate(
            flops=2 * count * weights.size,
            bytes_accessed=2 * weights.size,
            transcendentals=0,
        ),
    )(rows, weights)


def per_device(
    input_steps,
    gate_steps,
    conv_state,
    ssm_state,
    new_slot,
    remaining,
    conv_weight,
    conv_bias,
    coef_proj,
    delta_proj,
    delta_bias,
    decay_log,
    skip_gain,
    out_proj,
):
    groups = lax.axis_size("dp")
    my_group = lax.axis_index("dp")
    row_count, taps_kept, channels = conv_state.shape
    state_len = ssm_state.shape[1]
    steps_total = input_steps.shape[0]
    cap = row_count // groups
    total_rows = new_slot.shape[0]

    target = (new_slot // row_count).reshape(groups, row_count)
    position = jnp.arange(row_count, dtype=jnp.int32)
    earlier = position[None, :] < position[:, None]
    rank = jnp.sum(
        ((target[:, :, None] == target[:, None, :]) & earlier[None]).astype(jnp.int32), axis=2
    )
    source = jnp.broadcast_to(jnp.arange(groups, dtype=jnp.int32)[:, None], rank.shape)
    my_target = lax.dynamic_index_in_dim(target, my_group, 0, keepdims=False)
    my_rank = lax.dynamic_index_in_dim(rank, my_group, 0, keepdims=False)
    leave = jnp.where(
        my_rank < cap, my_target * cap + my_rank, row_count + my_rank - cap
    )
    slots = jnp.arange(row_count + cap, dtype=jnp.int32)
    send_index = jnp.sum(
        jnp.where(slots[:, None] == leave[None, :], position[None, :], 0), axis=1
    )
    arrive = jnp.where(rank < cap, source * cap + rank, row_count + rank - cap)
    here = (new_slot[None, :] == (my_group * row_count + position)[:, None])
    slot = jnp.sum(jnp.where(here, arrive.reshape(1, total_rows), 0), axis=1)
    remain_new = jnp.sum(jnp.where(here, remaining[None, :], 0), axis=1)
    group_ids = jnp.arange(groups, dtype=jnp.int32)
    is_extra = (rank == cap).reshape(1, total_rows)
    extra_from = jnp.sum(
        jnp.where(
            is_extra & (target.reshape(1, total_rows) == group_ids[:, None]),
            source.reshape(1, total_rows),
            0,
        ),
        axis=1,
    )

    def padded(rows, count):
        return jnp.pad(rows, ((0, 0),) * (rows.ndim - 2) + ((0, count - rows.shape[-2]), (0, 0)))

    ssm_base, ssm_extra = pack(send_index, ssm_state, groups)
    conv_packed = conv_state[send_index]
    ssm_rows, conv_rows = cap * state_len, cap * taps_kept
    depth = -(-(ssm_rows + conv_rows) // (16 * groups)) * 16
    extra = jnp.concatenate(
        [
            ssm_extra.reshape(ssm_rows, channels),
            conv_packed[row_count:].reshape(conv_rows, channels),
        ],
        axis=0,
    )
    pieces = padded(extra, groups * depth).reshape(groups, depth, channels)
    conv_depth = -(-conv_rows // 16) * 16
    conv_blocks = padded(
        conv_packed[:row_count].reshape(groups, conv_rows, channels), conv_depth
    )
    coef_width = coef_proj.shape[1]
    coef_depth = -(-coef_width // 16) * 16
    small = jnp.concatenate([padded(coef_proj.T, coef_depth), delta_proj], axis=0)
    ssm_base = lax.all_to_all(ssm_base, "dp", split_axis=0, concat_axis=0, tiled=True)
    extra, conv_base, small = move(
        extra_from,
        pieces,
        conv_blocks,
        small,
    )
    extra = extra.reshape(groups * depth, channels)
    ssm_extra = extra[:ssm_rows].reshape(cap, state_len, channels)
    conv_extra = extra[ssm_rows : ssm_rows + conv_rows].reshape(cap, taps_kept, channels)
    conv_base = conv_base[:, :conv_rows].reshape(row_count, taps_kept, channels)
    coef_whole = small[:, :coef_width].reshape(groups * coef_width, channels)
    delta_whole = small[:, coef_depth:].reshape(-1, channels)
    rank_len = delta_whole.shape[0]

    conv_moved = jnp.concatenate([conv_base, conv_extra], axis=0)[slot]
    sequence = [conv_moved[:, k] for k in range(taps_kept)]
    sequence += [input_steps[t] for t in range(steps_total)]
    wide = [entry.astype(jnp.float32) for entry in sequence]
    activated = jnp.stack(
        [
            jax.nn.silu(
                sum(wide[t + k] * conv_weight[k][None] for k in range(taps_kept + 1)) + conv_bias
            )
            for t in range(steps_total)
        ]
    )
    partial_value = lax.dot_general(
        activated.reshape(steps_total * row_count, channels).astype(jnp.bfloat16),
        coef_whole,
        (((1,), (1,)), ((), ())),
        preferred_element_type=jnp.float32,
    )
    partial_value, out_proj = lax.optimization_barrier(
        (partial_value.astype(jnp.bfloat16), out_proj)
    )
    out_whole = gather(out_proj, groups)
    low_rank = lax.psum(partial_value, "mp")
    coef = low_rank[:, rank_len:].astype(jnp.float32)
    coef = coef.reshape(steps_total, row_count, 2, state_len)
    coef = coef.transpose(1, 3, 0, 2).reshape(row_count, state_len, 2 * steps_total)
    active = remain_new[:, None] > jnp.arange(steps_total, dtype=jnp.int32)[None, :]
    step_size = jax.nn.softplus(
        jnp.dot(low_rank[:, :rank_len], delta_whole, preferred_element_type=jnp.float32)
        + delta_bias
    ).reshape(steps_total, row_count, channels)
    step_size = jnp.where(active.T[:, :, None], step_size, 0.0)

    decay_rate = -jnp.exp(decay_log)
    parts = 2
    layer_parts, final_parts = [], []
    for part in range(parts):
        mixed, final = scan(
            part,
            parts,
            slot,
            ssm_base,
            ssm_extra,
            step_size,
            activated,
            gate_steps,
            coef,
            active.astype(jnp.int32),
            decay_rate,
            skip_gain[None],
        )
        partial_mix = mix(mixed.reshape(-1, channels), out_whole)
        summed = lax.psum_scatter(partial_mix, "mp", scatter_dimension=1, tiled=True)
        layer_parts.append(summed.reshape(steps_total, row_count // parts, -1))
        final_parts.append(final)
    layer_out = jnp.concatenate(layer_parts, axis=1)
    ssm_final = jnp.concatenate(final_parts, axis=0)
    last = jnp.minimum(remain_new, steps_total)[:, None]
    window = []
    for k in range(taps_kept):
        entry = sequence[k]
        for t in range(1, steps_total + 1):
            entry = jnp.where(last == t, sequence[k + t], entry)
        window.append(entry)
    conv_final = jnp.stack(window, axis=1)
    return (layer_out, conv_final, ssm_final)


def solution(mesh):
    return jax.shard_map(
        per_device,
        mesh=mesh,
        in_specs=(
            P(None, "dp", "mp"),
            P(None, "dp", "mp"),
            P("dp", None, "mp"),
            P("dp", None, "mp"),
            P(),
            P(),
            P(None, "mp"),
            P("mp"),
            P("mp", "dp"),
            P("dp", "mp"),
            P("mp"),
            P(None, "mp"),
            P("mp"),
            P("mp", "dp"),
        ),
        out_specs=(P(None, "dp", "mp"), P("dp", None, "mp"), P("dp", None, "mp")),
        check_vma=False,
    )
```

```python
import functools

import jax
import jax.numpy as jnp
from jax import lax
from jax.experimental import pallas as pl
from jax.experimental.pallas import tpu as pltpu
from jax.sharding import PartitionSpec as P

VMEM_LIMIT = 48 * 1024 * 1024
CHUNKS = 4


def pack_kernel(index_ref, state_ref, base_ref, extra_ref):
    block = pl.program_id(0)
    cap = base_ref.shape[0]
    blocks = pl.num_programs(0)
    for i in range(cap):
        base_ref[i] = state_ref[index_ref[block * cap + i]]

    @pl.when(block == 0)
    def _():
        for i in range(cap):
            extra_ref[i] = state_ref[index_ref[blocks * cap + i]]


def pack(index, state, groups):
    rows, depth, channels = state.shape
    cap = rows // groups
    return pl.pallas_call(
        pack_kernel,
        out_shape=(
            jax.ShapeDtypeStruct((rows, depth, channels), state.dtype),
            jax.ShapeDtypeStruct((cap, depth, channels), state.dtype),
        ),
        grid_spec=pltpu.PrefetchScalarGridSpec(
            num_scalar_prefetch=1,
            grid=(groups,),
            in_specs=[
                pl.BlockSpec((rows, depth, channels), lambda i, _: (0, 0, 0)),
            ],
            out_specs=(
                pl.BlockSpec((cap, depth, channels), lambda i, _: (i, 0, 0)),
                pl.BlockSpec((cap, depth, channels), lambda i, _: (0, 0, 0)),
            ),
        ),
        compiler_params=pltpu.CompilerParams(vmem_limit_bytes=VMEM_LIMIT),
        cost_estimate=pl.CostEstimate(
            flops=0, bytes_accessed=4 * state.size, transcendentals=0
        ),
    )(index, state)


def scan_kernel(
    start,
    slot_ref,
    base_ref,
    extra_ref,
    step_ref,
    act_ref,
    gate_ref,
    coef_ref,
    mask_ref,
    decay_ref,
    skip_ref,
    mix_ref,
    final_ref,
    read_ref,
):
    first = (start + pl.program_id(0)) * step_ref.shape[1]
    rows_total = base_ref.shape[0]
    steps, rows, channels = step_ref.shape
    width = min(512, channels)

    def one_row(r, carry):
        slot = slot_ref[first + r]
        in_base = slot < rows_total
        at_base = jnp.minimum(slot, rows_total - 1)
        at_extra = jnp.maximum(slot - rows_total, 0)
        coef = coef_ref[r]
        for c in range(0, channels, width):
            cols = pl.ds(c, width)
            hidden = jnp.where(
                in_base,
                base_ref[at_base, :, cols].astype(jnp.float32),
                extra_ref[at_extra, :, cols].astype(jnp.float32),
            )
            decay = decay_ref[:, cols]
            for t in range(steps):
                step = step_ref[t, pl.ds(r, 1), cols]
                act = act_ref[t, pl.ds(r, 1), cols]
                hidden = (
                    jnp.exp(step * decay) * hidden + (step * act) * coef[:, 2 * t : 2 * t + 1]
                )
                read_ref[t, pl.ds(r, 1), cols] = jnp.sum(
                    hidden * coef[:, 2 * t + 1 : 2 * t + 2], axis=0, keepdims=True
                )
            final_ref[r, :, cols] = hidden.astype(final_ref.dtype)
        return carry

    lax.fori_loop(0, rows, one_row, 0)
    for t in range(steps):
        gate = gate_ref[t].astype(jnp.float32)
        mixer = (read_ref[t] + skip_ref[...] * act_ref[t]) * jax.nn.silu(gate)
        mix_ref[t] = jnp.where(mask_ref[:, t : t + 1] > 0, mixer, 0.0).astype(mix_ref.dtype)


def scan(part, parts, slot, base, extra, step, act, gate, coef, mask, decay, skip):
    rows, depth, channels = base.shape
    steps = step.shape[0]
    tile = 16
    count = rows // parts
    start = part * count // tile
    cap = extra.shape[0]

    def whole(shape):
        return pl.BlockSpec(shape, lambda i, _: (0,) * len(shape))

    per_step = pl.BlockSpec((steps, tile, channels), lambda i, _: (0, start + i, 0))
    return pl.pallas_call(
        functools.partial(scan_kernel, start),
        out_shape=(
            jax.ShapeDtypeStruct((steps, count, channels), jnp.bfloat16),
            jax.ShapeDtypeStruct((count, depth, channels), jnp.bfloat16),
        ),
        grid_spec=pltpu.PrefetchScalarGridSpec(
            num_scalar_prefetch=1,
            grid=(count // tile,),
            in_specs=[
                whole((rows, depth, channels)),
                whole((cap, depth, channels)),
                per_step,
                per_step,
                per_step,
                pl.BlockSpec((tile, depth, 2 * steps), lambda i, _: (start + i, 0, 0)),
                pl.BlockSpec((tile, steps), lambda i, _: (start + i, 0)),
                whole((depth, channels)),
                whole((1, channels)),
            ],
            out_specs=(
                pl.BlockSpec((steps, tile, channels), lambda i, _: (0, i, 0)),
                pl.BlockSpec((tile, depth, channels), lambda i, _: (i, 0, 0)),
            ),
            scratch_shapes=[pltpu.VMEM((steps, tile, channels), jnp.float32)],
        ),
        compiler_params=pltpu.CompilerParams(vmem_limit_bytes=VMEM_LIMIT),
        cost_estimate=pl.CostEstimate(
            flops=8 * steps * base.size // parts,
            bytes_accessed=4 * base.size + 16 * step.size,
            transcendentals=steps * base.size // parts,
        ),
    )(slot, base, extra, step, act, gate, coef, mask, decay, skip)


def remote(src, dst, send_sem, recv_sem, peer):
    return pltpu.make_async_remote_copy(
        src_ref=src,
        dst_ref=dst,
        send_sem=send_sem,
        recv_sem=recv_sem,
        device_id={"dp": peer},
        device_id_type=pl.DeviceIdType.MESH,
    )


def greet(groups):
    me = lax.axis_index("dp")
    barrier = pltpu.get_barrier_semaphore()
    for k in range(1, groups):
        pl.semaphore_signal(
            barrier,
            inc=1,
            device_id={"dp": (me + k) % groups},
            device_id_type=pl.DeviceIdType.MESH,
        )
    pl.semaphore_wait(barrier, groups - 1)


def gather_blocks(groups, inner, parts, own_sem, send_sem, recv_sem, between):
    me = lax.axis_index("dp")
    outer = groups // inner
    mine_z = me // inner
    mine_x = me % inner

    def copy_of(kind, src, dst, origin, lane, peer):
        return remote(
            src, dst.at[origin], send_sem.at[kind, origin, lane], recv_sem.at[kind, origin], peer
        )

    def forward(kind, src, dst, origin, ups):
        for up in ups:
            peer = me + inner if up else me - inner
            room = mine_z + 1 < outer if up else mine_z >= 1

            @pl.when(room)
            def _():
                copy_of(kind, src, dst, origin, 0 if up else 1, peer).start()

        for k in range(1, inner):
            peer = mine_z * inner + (mine_x + k) % inner
            copy_of(kind, src, dst, origin, 1 + k, peer).start()

    def arrived(kind, dst, origin):
        copy_of(kind, dst.at[origin], dst, origin, 0, me).wait_recv()

    own = []
    for kind, (src, dst) in enumerate(parts):
        forward(kind, src, dst, me, (True, False))
        copy = pltpu.make_async_copy(src, dst.at[me], own_sem.at[kind])
        copy.start()
        own.append(copy)
    between()
    for s in range(1, outer):
        for kind, (_, dst) in enumerate(parts):
            for up in (True, False):
                origin = me - s * inner if up else me + s * inner
                there = mine_z >= s if up else mine_z + s < outer

                @pl.when(there)
                def _():
                    arrived(kind, dst, origin)
                    forward(kind, dst.at[origin], dst, origin, (up,))

    for kind, (src, dst) in enumerate(parts):
        for z in range(outer):
            for k in range(1, inner):
                arrived(kind, dst, z * inner + (mine_x + k) % inner)
        own[kind].wait()
        for z in range(outer):
            origin = z * inner + mine_x

            @pl.when((mine_z >= z) & (mine_z + 1 < outer))
            def _():
                copy_of(kind, src, dst, origin, 0, me).wait_send()

            @pl.when((mine_z <= z) & (mine_z >= 1))
            def _():
                copy_of(kind, src, dst, origin, 1, me).wait_send()

            for k in range(1, inner):
                copy_of(kind, src, dst, origin, 1 + k, me).wait_send()


def move_kernel(
    groups,
    inner,
    from_ref,
    piece_ref,
    conv_ref,
    small_ref,
    piece_out,
    conv_out,
    small_all,
    held,
    passed,
    own_sem,
    send_sem,
    recv_sem,
    gather_own,
    gather_send,
    gather_recv,
):
    me = lax.axis_index("dp")
    greet(groups)

    def exchange(kind, src, dst):
        copies = []
        for k in range(1, groups):
            peer = (me + k) % groups
            copy = remote(
                src.at[peer], dst.at[me], send_sem.at[kind, k], recv_sem.at[kind, k], peer
            )
            copy.start()
            copies.append(copy)
        own = pltpu.make_async_copy(src.at[me], dst.at[me], own_sem.at[kind])
        own.start()
        return copies, own

    def finish(started):
        copies, own = started
        for copy in copies:
            copy.wait_recv()
        own.wait()

    first = exchange(0, piece_ref, held)
    conv = exchange(1, conv_ref, conv_out)
    second = []

    def pass_on():
        finish(first)
        for h in range(groups):
            passed[h] = held[from_ref[h]]
        second.append(exchange(2, passed, piece_out))

    gather_blocks(
        groups, inner, [(small_ref, small_all)], gather_own, gather_send, gather_recv, pass_on
    )
    finish(conv)
    finish(second[0])
    for copies, _ in (first, conv, second[0]):
        for copy in copies:
            copy.wait_send()


def gather_kernel(groups, inner, src_ref, all_ref, own_sem, send_sem, recv_sem):
    greet(groups)
    depth = src_ref.shape[0] // CHUNKS
    parts = [
        (src_ref.at[pl.ds(c * depth, depth)], all_ref.at[:, pl.ds(c * depth, depth)])
        for c in range(CHUNKS)
    ]
    gather_blocks(groups, inner, parts, own_sem, send_sem, recv_sem, lambda: None)


def inner_of(groups):
    inner = 1
    while inner * inner * 4 <= groups:
        inner *= 2
    return inner


def gather_scratch(kinds, groups, inner):
    return [
        pltpu.SemaphoreType.DMA((kinds,)),
        pltpu.SemaphoreType.DMA((kinds, groups, 1 + inner)),
        pltpu.SemaphoreType.DMA((kinds, groups)),
    ]


def move(extra_from, pieces, conv, small):
    groups = pieces.shape[0]
    inner = inner_of(groups)
    held = pl.BlockSpec(memory_space=pl.ANY)

    def like(array):
        return jax.ShapeDtypeStruct(array.shape, array.dtype)

    return pl.pallas_call(
        functools.partial(move_kernel, groups, inner),
        out_shape=(
            like(pieces),
            like(conv),
            jax.ShapeDtypeStruct((groups,) + small.shape, small.dtype),
        ),
        in_specs=[pl.BlockSpec(memory_space=pltpu.SMEM)] + [held] * 3,
        out_specs=(held,) * 3,
        scratch_shapes=[
            pltpu.VMEM(pieces.shape, pieces.dtype),
            pltpu.VMEM(pieces.shape, pieces.dtype),
            pltpu.SemaphoreType.DMA((3,)),
            pltpu.SemaphoreType.DMA((3, groups)),
            pltpu.SemaphoreType.DMA((3, groups)),
        ]
        + gather_scratch(1, groups, inner),
        compiler_params=pltpu.CompilerParams(collective_id=0, has_side_effects=True),
        cost_estimate=pl.CostEstimate(
            flops=0, bytes_accessed=64 * groups * small.size, transcendentals=0
        ),
    )(extra_from, pieces, conv, small)


def gather(block, groups):
    inner = inner_of(groups)
    held = pl.BlockSpec(memory_space=pl.ANY)
    return pl.pallas_call(
        functools.partial(gather_kernel, groups, inner),
        out_shape=jax.ShapeDtypeStruct((groups,) + block.shape, block.dtype),
        in_specs=[held],
        out_specs=held,
        scratch_shapes=gather_scratch(CHUNKS, groups, inner),
        compiler_params=pltpu.CompilerParams(collective_id=1, has_side_effects=True),
        cost_estimate=pl.CostEstimate(
            flops=0, bytes_accessed=32 * groups * block.size, transcendentals=0
        ),
    )(block)


def mix_kernel(rows_ref, weight_ref, out_ref):
    out_ref[...] = jnp.dot(
        rows_ref[...], weight_ref[0], preferred_element_type=jnp.float32
    ).astype(out_ref.dtype)


def mix(rows, weights):
    groups, channels, width = weights.shape
    count = rows.shape[0]
    return pl.pallas_call(
        mix_kernel,
        out_shape=jax.ShapeDtypeStruct((count, groups * width), jnp.bfloat16),
        grid=(groups,),
        in_specs=[
            pl.BlockSpec((count, channels), lambda g: (0, 0)),
            pl.BlockSpec((1, channels, width), lambda g: (g, 0, 0)),
        ],
        out_specs=pl.BlockSpec((count, width), lambda g: (0, g)),
        compiler_params=pltpu.CompilerParams(vmem_limit_bytes=VMEM_LIMIT),
        cost_estimate=pl.CostEstimate(
            flops=2 * count * weights.size,
            bytes_accessed=2 * weights.size,
            transcendentals=0,
        ),
    )(rows, weights)


def per_device(
    input_steps,
    gate_steps,
    conv_state,
    ssm_state,
    new_slot,
    remaining,
    conv_weight,
    conv_bias,
    coef_proj,
    delta_proj,
    delta_bias,
    decay_log,
    skip_gain,
    out_proj,
):
    groups = lax.axis_size("dp")
    my_group = lax.axis_index("dp")
    row_count, taps_kept, channels = conv_state.shape
    state_len = ssm_state.shape[1]
    steps_total = input_steps.shape[0]
    cap = row_count // groups
    total_rows = new_slot.shape[0]

    target = (new_slot // row_count).reshape(groups, row_count)
    position = jnp.arange(row_count, dtype=jnp.int32)
    earlier = position[None, :] < position[:, None]
    rank = jnp.sum(
        ((target[:, :, None] == target[:, None, :]) & earlier[None]).astype(jnp.int32), axis=2
    )
    source = jnp.broadcast_to(jnp.arange(groups, dtype=jnp.int32)[:, None], rank.shape)
    my_target = lax.dynamic_index_in_dim(target, my_group, 0, keepdims=False)
    my_rank = lax.dynamic_index_in_dim(rank, my_group, 0, keepdims=False)
    leave = jnp.where(
        my_rank < cap, my_target * cap + my_rank, row_count + my_rank - cap
    )
    slots = jnp.arange(row_count + cap, dtype=jnp.int32)
    send_index = jnp.sum(
        jnp.where(slots[:, None] == leave[None, :], position[None, :], 0), axis=1
    )
    arrive = jnp.where(rank < cap, source * cap + rank, row_count + rank - cap)
    here = (new_slot[None, :] == (my_group * row_count + position)[:, None])
    slot = jnp.sum(jnp.where(here, arrive.reshape(1, total_rows), 0), axis=1)
    remain_new = jnp.sum(jnp.where(here, remaining[None, :], 0), axis=1)
    group_ids = jnp.arange(groups, dtype=jnp.int32)
    is_extra = (rank == cap).reshape(1, total_rows)
    extra_from = jnp.sum(
        jnp.where(
            is_extra & (target.reshape(1, total_rows) == group_ids[:, None]),
            source.reshape(1, total_rows),
            0,
        ),
        axis=1,
    )

    def padded(rows, count):
        return jnp.pad(rows, ((0, 0),) * (rows.ndim - 2) + ((0, count - rows.shape[-2]), (0, 0)))

    ssm_base, ssm_extra = pack(send_index, ssm_state, groups)
    conv_packed = conv_state[send_index]
    ssm_rows, conv_rows = cap * state_len, cap * taps_kept
    depth = -(-(ssm_rows + conv_rows) // (16 * groups)) * 16
    extra = jnp.concatenate(
        [
            ssm_extra.reshape(ssm_rows, channels),
            conv_packed[row_count:].reshape(conv_rows, channels),
        ],
        axis=0,
    )
    pieces = padded(extra, groups * depth).reshape(groups, depth, channels)
    conv_depth = -(-conv_rows // 16) * 16
    conv_blocks = padded(
        conv_packed[:row_count].reshape(groups, conv_rows, channels), conv_depth
    )
    coef_width = coef_proj.shape[1]
    coef_depth = -(-coef_width // 16) * 16
    small = jnp.concatenate([padded(coef_proj.T, coef_depth), delta_proj], axis=0)
    extra, conv_base, small = move(
        extra_from,
        pieces,
        conv_blocks,
        small,
    )
    ssm_base, extra = lax.optimization_barrier((ssm_base, extra))
    ssm_base = lax.all_to_all(ssm_base, "dp", split_axis=0, concat_axis=0, tiled=True)
    extra = extra.reshape(groups * depth, channels)
    ssm_extra = extra[:ssm_rows].reshape(cap, state_len, channels)
    conv_extra = extra[ssm_rows : ssm_rows + conv_rows].reshape(cap, taps_kept, channels)
    conv_base = conv_base[:, :conv_rows].reshape(row_count, taps_kept, channels)
    coef_whole = small[:, :coef_width].reshape(groups * coef_width, channels)
    delta_whole = small[:, coef_depth:].reshape(-1, channels)
    rank_len = delta_whole.shape[0]

    conv_moved = jnp.concatenate([conv_base, conv_extra], axis=0)[slot]
    sequence = [conv_moved[:, k] for k in range(taps_kept)]
    sequence += [input_steps[t] for t in range(steps_total)]
    wide = [entry.astype(jnp.float32) for entry in sequence]
    activated = jnp.stack(
        [
            jax.nn.silu(
                sum(wide[t + k] * conv_weight[k][None] for k in range(taps_kept + 1)) + conv_bias
            )
            for t in range(steps_total)
        ]
    )
    partial_value = lax.dot_general(
        activated.reshape(steps_total * row_count, channels).astype(jnp.bfloat16),
        coef_whole,
        (((1,), (1,)), ((), ())),
        preferred_element_type=jnp.float32,
    )
    partial_value, out_proj = lax.optimization_barrier(
        (partial_value.astype(jnp.bfloat16), out_proj)
    )
    out_whole = gather(out_proj, groups)
    low_rank = lax.psum(partial_value, "mp")
    coef = low_rank[:, rank_len:].astype(jnp.float32)
    coef = coef.reshape(steps_total, row_count, 2, state_len)
    coef = coef.transpose(1, 3, 0, 2).reshape(row_count, state_len, 2 * steps_total)
    active = remain_new[:, None] > jnp.arange(steps_total, dtype=jnp.int32)[None, :]
    step_size = jax.nn.softplus(
        jnp.dot(low_rank[:, :rank_len], delta_whole, preferred_element_type=jnp.float32)
        + delta_bias
    ).reshape(steps_total, row_count, channels)
    step_size = jnp.where(active.T[:, :, None], step_size, 0.0)

    decay_rate = -jnp.exp(decay_log)
    parts = 2
    layer_parts, final_parts = [], []
    for part in range(parts):
        mixed, final = scan(
            part,
            parts,
            slot,
            ssm_base,
            ssm_extra,
            step_size,
            activated,
            gate_steps,
            coef,
            active.astype(jnp.int32),
            decay_rate,
            skip_gain[None],
        )
        partial_mix = mix(mixed.reshape(-1, channels), out_whole)
        summed = lax.psum_scatter(partial_mix, "mp", scatter_dimension=1, tiled=True)
        layer_parts.append(summed.reshape(steps_total, row_count // parts, -1))
        final_parts.append(final)
    layer_out = jnp.concatenate(layer_parts, axis=1)
    ssm_final = jnp.concatenate(final_parts, axis=0)
    last = jnp.minimum(remain_new, steps_total)[:, None]
    window = []
    for k in range(taps_kept):
        entry = sequence[k]
        for t in range(1, steps_total + 1):
            entry = jnp.where(last == t, sequence[k + t], entry)
        window.append(entry)
    conv_final = jnp.stack(window, axis=1)
    return (layer_out, conv_final, ssm_final)


def solution(mesh):
    return jax.shard_map(
        per_device,
        mesh=mesh,
        in_specs=(
            P(None, "dp", "mp"),
            P(None, "dp", "mp"),
            P("dp", None, "mp"),
            P("dp", None, "mp"),
            P(),
            P(),
            P(None, "mp"),
            P("mp"),
            P("mp", "dp"),
            P("dp", "mp"),
            P("mp"),
            P(None, "mp"),
            P("mp"),
            P("mp", "dp"),
        ),
        out_specs=(P(None, "dp", "mp"), P("dp", None, "mp"), P("dp", None, "mp")),
        check_vma=False,
    )
```
